32 devices in a mesh: shot: 8 (over z, core), dom: 4 (over y, x).
Axes of the slice: x: 2, y: 2, z: 4, core: 2. Of those that a mesh axis runs over, the one named last changes fastest.
Arguments:
- kappa: float32 [8, 512, 128], P('dom'), may hold values from 0.05 to 0.15
- wave_now: float32 [8, 8, 512, 128], P('shot', 'dom'), may hold values from -6 to 6
- wave_before: float32 [8, 8, 512, 128], P('shot', 'dom'), may hold values from -6 to 6
- wavelet: float32 [8, 4], P('shot'), may hold values from -8 to 8
- source_cell: int32 [8], P('shot'), may hold values from 0 to 524287
- receiver_cells: int32 [8, 2048], P('shot'), may hold values from 0 to 524287
- observed: float32 [8, 4, 2048], P('shot'), may hold values from -6 to 6
Outputs:
- total_gradient: float32 [8, 512, 128], P('dom', 'shot')
- wave_next: float32 [8, 8, 512, 128], P('shot', 'dom')
The draws below stay inside these ranges and needn't reach their ends.
Inputs may be any that keep to these rules, and one draw needn't show every extreme that they name: `source_cell`: a cell index x * 512 * 128 + y * 128 + z. `receiver_cells`: cell indices x * 512 * 128 + y * 128 + z; a cell may hold several receivers.
All inputs are finite; a program needn't handle non-finite values.
Results may differ from the reference program's by a relative error of at most 0.00013.
Values sent between devices are 32-bit elements; how exact they have to be, the bound alone decides.
No kernel may reach another device: no remote copies, remote signals or barrier semaphores. Data moves between devices by JAX's collectives and lax.ppermute only.
A program may use at most 64 MiB of HBM per device.

```python
import jax
import jax.numpy as jnp
from jax import lax

NY = 512
NZ = 128
NREC = 2048
NT = 4
NX = 8
SHOTS = 8


def plant(array, key, smallest, largest):
    dims = array.shape
    spot = [jax.random.randint(jax.random.fold_in(key, axis), (), 0, dims[axis]) for axis in range(len(dims))]
    array = array.at[tuple(spot)].set(smallest)
    longest = dims.index(max(dims))
    spot[longest] = (spot[longest] + 1) % dims[longest]
    return array.at[tuple(spot)].set(largest)


def levels(own_key, dims, cuts, least, high):
    gain = 1.0
    for dim, shards_of in cuts:
        heights = jax.random.uniform(jax.random.fold_in(jax.random.fold_in(own_key, 6), dim), (shards_of,), jnp.float32, least / len(cuts), high / len(cuts))
        gain = gain * jnp.repeat(jnp.exp(heights), dims[dim] // shards_of).reshape((-1,) + (1,) * (len(dims) - 1 - dim))
    return gain


def gaussian(own_key, extent, spread, most, cuts=(), held_as=jnp.bfloat16):
    drawn = jax.random.normal(own_key, extent, jnp.float32) * spread
    if len(cuts) > 0:
        drawn = levels(own_key, extent, cuts, -0.22, 0.18) * drawn
    return jnp.clip(drawn, min=-most, max=most).astype(held_as)


def setup_inputs(seed: int = 0) -> dict:
    arg_keys = jax.random.split(jax.random.key(seed), 8)
    kappa = jnp.clip(0.05 + 0.10000001 * jax.random.uniform(arg_keys[0], (NX, NY, NZ), jnp.float32) ** levels(arg_keys[0], (NX, NY, NZ), ((0, 4),), -0.2, 0.2), 0.05, 0.15)
    wave_now = gaussian(arg_keys[1], (SHOTS, NX, NY, NZ), 1.0, 6.0, ((0, 8), (1, 4)), jnp.float32)
    wave_before = gaussian(arg_keys[2], (SHOTS, NX, NY, NZ), 1.0, 6.0, ((0, 8), (1, 4)), jnp.float32)
    wavelet = gaussian(arg_keys[3], (SHOTS, NT), 2.0, 8.0, ((0, 8),), jnp.float32)
    source_cell = plant(jax.random.randint(arg_keys[4], (SHOTS,), 0, NX * NY * NZ), jax.random.fold_in(arg_keys[4], 1), 0, (NX * NY * NZ) - 1).astype(jnp.int32)
    receiver_cells = plant(jax.random.randint(arg_keys[5], (SHOTS, NREC), 0, NX * NY * NZ), jax.random.fold_in(arg_keys[5], 1), 0, (NX * NY * NZ) - 1).astype(jnp.int32)
    observed = gaussian(arg_keys[6], (SHOTS, NT, NREC), 1.0, 6.0, ((0, 8),), jnp.float32)
    return {"kappa": kappa, "wave_now": wave_now, "wave_before": wave_before, "wavelet": wavelet, "source_cell": source_cell, "receiver_cells": receiver_cells, "observed": observed}


PRIOR_GAIN = 50.0

def neighbours(padded):
    core = padded[..., 1:-1, :, :]
    widths = [(0, 0)] * (core.ndim - 2) + [(1, 1), (1, 1)]
    flank = jnp.pad(core, widths)
    total = padded[..., 2:, :, :] + padded[..., :-2, :, :]
    total = total + flank[..., 2:, 1:-1] + flank[..., :-2, 1:-1]
    total = total + flank[..., 1:-1, 2:] + flank[..., 1:-1, :-2]
    return total

def laplace(field):
    padded = jnp.pad(field, ((1, 1), (0, 0), (0, 0)))
    return neighbours(padded) - 6.0 * field

def reference(kappa, wave_now, wave_before, wavelet, source_cell, receiver_cells, observed):

    def one_shot(total, items):
        start_now, start_before, pulse, source, receivers, recorded = items

        def misfit(model):
            now, before = (start_now, start_before)
            value = jnp.zeros((), model.dtype)
            for step in range(NT):
                lap = laplace(now)
                after = 2.0 * now - before + model * lap
                after = after.reshape(-1).at[source].add(pulse[step]).reshape(now.shape)
                miss = after.reshape(-1)[receivers] - recorded[step]
                value = value + 0.5 * jnp.sum(miss * miss)
                before, now = (now, after)
            return (value, now)
        value, pull, final = jax.vjp(misfit, kappa, has_aux=True)
        image, = pull(jnp.ones_like(value))
        return (total + image, final)
    image, wave_next = lax.scan(one_shot, jnp.zeros_like(kappa), (wave_now, wave_before, wavelet, source_cell, receiver_cells, observed))
    padded_model = jnp.pad(kappa, ((1, 1), (0, 0), (0, 0)))
    smooth = neighbours(padded_model) / 6.0
    score = (smooth - kappa) * PRIOR_GAIN
    total_gradient = image / NT - score
    return (total_gradient, wave_next)
```

```python
import functools

import jax
import jax.numpy as jnp
from jax import lax
from jax.experimental import pallas as pl
from jax.experimental.pallas import tpu as pltpu
from jax.sharding import PartitionSpec as P

NT = 4
PRIOR_GAIN = 50.0
EDGE = 8
VMEM = pl.BlockSpec(memory_space=pltpu.VMEM)
SMEM = pl.BlockSpec(memory_space=pltpu.SMEM)
LIMIT = 48 * 1024 * 1024


def call(body, out_rows, scratch=(), in_specs=(), flops=0, moved=0):
    return pl.pallas_call(
        body,
        out_shape=[jax.ShapeDtypeStruct(s, jnp.float32) for s in out_rows],
        in_specs=list(in_specs),
        out_specs=[VMEM] * len(out_rows),
        scratch_shapes=list(scratch),
        compiler_params=pltpu.CompilerParams(vmem_limit_bytes=LIMIT),
        cost_estimate=pl.CostEstimate(flops=flops, bytes_accessed=moved, transcendentals=0),
    )


def window(field, plane, block, blocks, rows):
    first = pl.multiple_of(block * rows, 8)
    above = pl.multiple_of(jnp.maximum(first - EDGE, 0), 8)
    below = pl.multiple_of(jnp.minimum(first + rows, (blocks * rows) - EDGE), 8)
    top = field[plane, pl.ds(above, EDGE), :]
    bottom = field[plane, pl.ds(below, EDGE), :]
    top = jnp.where(block > 0, top, 0.0)
    bottom = jnp.where(block < blocks - 1, bottom, 0.0)
    return top, field[plane, pl.ds(first, rows), :], bottom


def pack(blocks, planes, rows, *refs):
    fields, outs = refs[: len(refs) - blocks], refs[len(refs) - blocks :]
    dom = lax.axis_index("dom")
    tall = rows + 2 * EDGE
    for s in range(blocks):
        block = lax.bitwise_xor(dom, s)
        for f, field in enumerate(fields):
            for p in range(planes):
                top, core, bottom = window(field, p, block, blocks, rows)
                at = (f * planes + p) * tall
                outs[s][at : at + EDGE, :] = top
                outs[s][at + EDGE : at + EDGE + rows, :] = core
                outs[s][at + EDGE + rows : at + tall, :] = bottom


def spread(depth, ny, rows, count, cells_ref, observed_ref, count_ref, *rest):
    outs, (value, picks) = rest[:NT], rest[NT:]
    tall = rows + 2 * EDGE
    planes = count_ref.shape[0] // tall
    dom = lax.axis_index("dom")
    cells = cells_ref[...]
    line = cells // depth
    x = line // ny
    y = line - x * ny - (dom * rows - EDGE)
    row = jnp.where((y >= 0) & (y < tall), x * tall + y, -1)
    lane = (cells - line * depth).astype(jnp.float32)
    picks[...] = row
    stack = jnp.concatenate([lane, observed_ref[0], jnp.zeros((3, count), jnp.float32)], axis=0)
    columns = 128
    for j in range(count // columns):
        turned = stack[:, j * columns : (j + 1) * columns].T
        hot = lax.broadcasted_iota(jnp.int32, (columns, depth), 1).astype(jnp.float32) == turned[:, 0:1]
        at = slice(j * columns, (j + 1) * columns)
        value[at, 0:depth] = jnp.where(hot, 1.0, 0.0).astype(jnp.bfloat16)
        for n in range(NT):
            left = jnp.where(hot, turned[:, n + 1 : n + 2], 0.0)
            for part in range(3):
                piece = left.astype(jnp.bfloat16)
                left = left - piece.astype(jnp.float32)
                to = (1 + 3 * n + part) * depth
                value[at, to : to + depth] = piece
    some = tall * 2

    def chunk(i, _):
        first = pl.multiple_of(i * some, 8)
        ids = lax.broadcasted_iota(jnp.int32, (some, count), 0) + first
        hot = jnp.where(ids == picks[...], 1.0, 0.0).astype(jnp.bfloat16)
        out = jnp.dot(hot, value[...], preferred_element_type=jnp.float32)
        count_ref[pl.ds(first, some), :] = out[:, 0:depth]
        for n in range(NT):
            at = (1 + 3 * n) * depth
            total = out[:, at + depth : at + 2 * depth] + out[:, at + 2 * depth : at + 3 * depth]
            outs[n][pl.ds(first, some), :] = out[:, at : at + depth] + total
        return 0

    lax.fori_loop(0, planes // 2, chunk, 0)


def sixth(field, x, first, some, low, high):
    mid = field[x, first : first + some, :]
    total = field[x + 1, first : first + some, :] + field[x - 1, first : first + some, :]
    total = total + (field[x, first + 1 : first + some + 1, :] + field[x, first - 1 : first + some - 1, :])
    up = jnp.where(high, 0.0, pltpu.roll(mid, mid.shape[1] - 1, 1))
    down = jnp.where(low, 0.0, pltpu.roll(mid, 1, 1))
    return total + (up + down), mid


def steps(blocks, planes, rows, depth, ny, *refs):
    refs = list(refs)
    source, wavelet = refs[:2]
    early = refs[2 : 2 + blocks]
    late = refs[2 + blocks : 2 + 2 * blocks]
    count = refs[2 + 2 * blocks]
    heard = refs[3 + 2 * blocks : 3 + NT + 2 * blocks]
    refs = refs[3 + NT + 2 * blocks :]
    turned, (keep, give) = refs[:blocks], refs[blocks : blocks + 2]
    refs = refs[blocks + 2 :]
    wave, refs = refs[: NT + 1], refs[NT + 1 :]
    lap, refs = refs[:NT], refs[NT:]
    before, model, image = refs[:3]
    adjoint = refs[3:6]
    weighted = refs[6:8]
    tall = rows + 2 * EDGE
    nx = blocks * planes
    dom = lax.axis_index("dom")
    shot = lax.axis_index("shot")
    core = lax.rem(shot, 2)

    zero_plane = jnp.zeros((tall + 16, depth), jnp.float32)
    zero_edge = jnp.zeros((8, depth), jnp.float32)
    for field in (*wave, model, *weighted):
        field[0] = zero_plane
        field[nx + 1] = zero_plane
        for x in range(1, nx + 1):
            field[x, 0:8, :] = zero_edge
            field[x, 8 + tall : 16 + tall, :] = zero_edge
    for s in range(blocks):
        first = planes * lax.bitwise_xor(dom, s)
        for p in range(planes):
            at = slice(p * tall, (p + 1) * tall)
            wave[0][1 + first + p, 8 : 8 + tall, :] = early[s][at, :]
            more = slice((planes + p) * tall, (planes + p + 1) * tall)
            model[1 + first + p, 8 : 8 + tall, :] = early[s][more, :]
            before[first + p] = late[s][at, :]

    some = 48
    lanes = lax.broadcasted_iota(jnp.int32, (some, depth), 1)
    low, high = lanes == 0, lanes == depth - 1

    line = source[0] // depth
    spot = source[0] - line * depth
    sx = line // ny
    sy = line - sx * ny - (dom * rows - EDGE)
    source_here = (sy >= 0) & (sy < tall)
    sy = jnp.clip(sy, 0, tall - 1)
    source_lane = lax.broadcasted_iota(jnp.int32, (1, depth), 1) == spot

    for n in range(NT):

        def forward(x, _, n=n):
            for a in range(0, tall, some):
                total, mid = sixth(wave[n], x + 1, 8 + a, some, low, high)
                bend = total - 6.0 * mid
                lap[n][x, a : a + some, :] = bend
                old = before[x, a : a + some, :] if n == 0 else wave[n - 1][x + 1, 8 + a : 8 + a + some, :]
                new = 2.0 * mid - old + model[x + 1, 8 + a : 8 + a + some, :] * bend
                wave[n + 1][x + 1, 8 + a : 8 + a + some, :] = new
            return 0

        lax.fori_loop(0, nx, forward, 0)

        @pl.when(source_here)
        def _():
            row = wave[n + 1][sx + 1, pl.ds(8 + sy, 1), :]
            wave[n + 1][sx + 1, pl.ds(8 + sy, 1), :] = row + jnp.where(source_lane, wavelet[0, n], 0.0)

    for s in range(blocks):
        first = planes * lax.bitwise_xor(dom, s)
        for p in range(planes):
            turned[s][p * rows : (p + 1) * rows, :] = wave[NT][1 + first + p, 8 + EDGE : 8 + EDGE + rows, :]

    for level in range(NT, 0, -1):
        now, after, last = adjoint[level % 3], adjoint[(level + 1) % 3], adjoint[(level + 2) % 3]
        push, pull = weighted[level % 2], weighted[(level + 1) % 2]

        def backward(x, _, level=level, now=now, after=after, last=last, push=push, pull=pull):
            for a in range(0, tall, some):
                at = pl.ds(pl.multiple_of(x * tall + a, 8), some)
                miss = count[at, :] * wave[level][x + 1, 8 + a : 8 + a + some, :] - heard[level - 1][at, :]
                if level < NT:
                    total, mid = sixth(pull, x + 1, 8 + a, some, low, high)
                    miss = miss + 2.0 * after[x, a : a + some, :] + (total - 6.0 * mid)
                if level < NT - 1:
                    miss = miss - last[x, a : a + some, :]
                if level > 1:
                    now[x, a : a + some, :] = miss
                    push[x + 1, 8 + a : 8 + a + some, :] = miss * model[x + 1, 8 + a : 8 + a + some, :]
                part = miss * lap[level - 1][x, a : a + some, :]
                if level < NT:
                    part = part + image[x, a : a + some, :]
                if level == 1:
                    total, mid = sixth(model, x + 1, 8 + a, some, low, high)
                    score = (total / 6.0 - mid) * PRIOR_GAIN
                    part = part / NT - jnp.where(shot == 0, score, 0.0)
                image[x, a : a + some, :] = part
            return 0

        lax.fori_loop(0, nx, backward, 0)

    half = rows // 2
    mine = pl.multiple_of(EDGE + core * half, 8)
    mates = pl.multiple_of(EDGE + (1 - core) * half, 8)
    for x in range(nx):
        keep[x * half : (x + 1) * half, :] = image[x, pl.ds(mine, half), :]
        give[x * half : (x + 1) * half, :] = image[x, pl.ds(mates, half), :]


def cut(blocks, keep, got, *outs):
    dom = lax.axis_index("dom")
    size = outs[0].shape[0]
    for s in range(blocks):
        at = pl.ds(pl.multiple_of(lax.bitwise_xor(dom, s) * size, 8), size)
        outs[s][...] = keep[at, :] + got[at, :]


def sort(blocks, *refs):
    came, outs, held = refs[:blocks], refs[blocks : 2 * blocks], refs[2 * blocks]
    dom, pair = lax.axis_index("dom"), lax.axis_index("shot") // 2
    for s in range(blocks):
        held[lax.bitwise_xor(dom, s)] = came[s][...]
    for s in range(blocks):
        outs[s][...] = held[lax.bitwise_xor(pair, s)]


def add(planes, *refs):
    out = refs[-1]
    size = out.shape[1]
    for p in range(planes):
        total = refs[0][p * size : (p + 1) * size, :]
        for ref in refs[1:-1]:
            total = total + ref[p * size : (p + 1) * size, :]
        out[p] = total


def join(planes, rows, *refs):
    out = refs[-1]
    dom = lax.axis_index("dom")
    for s, ref in enumerate(refs[:-1]):
        at = pl.ds(pl.multiple_of(lax.bitwise_xor(dom, s) * rows, 8), rows)
        for p in range(planes):
            out[p, at, :] = ref[p * rows : (p + 1) * rows, :]


def shards(kappa, wave_now, wave_before, wavelet, source_cell, receiver_cells, observed):
    shots, blocks = lax.axis_size("shot"), lax.axis_size("dom")
    _, planes, ny, depth = wave_now.shape
    rows = ny // blocks
    tall = rows + 2 * EDGE
    nx = planes * blocks
    listed = receiver_cells.shape[1]

    def across(array, to):
        pairs = []
        for shot in range(shots):
            for dom in range(blocks):
                there = to(shot, dom)
                pairs.append((shot * blocks + dom, there[0] * blocks + there[1]))
        return lax.ppermute(array, ("shot", "dom"), pairs)

    def over_dom(arrays):
        return [arrays[0]] + [across(arrays[s], lambda shot, dom, s=s: (shot, dom ^ s)) for s in range(1, blocks)]

    def over_pairs(arrays):
        return [arrays[0]] + [across(arrays[s], lambda shot, dom, s=s: (shot ^ (2 * s), dom)) for s in range(1, blocks)]

    packed = functools.partial(pack, blocks, planes, rows)
    now, before = wave_now[0], wave_before[0]
    early = call(packed, [(2 * planes * tall, depth)] * blocks, in_specs=[VMEM] * 2)(now, kappa)
    late = call(packed, [(planes * tall, depth)] * blocks, in_specs=[VMEM])(before)
    early, late = over_dom(early), over_dom(late)

    wide = (1 + 3 * NT) * depth
    heard = call(
        functools.partial(spread, depth, ny, rows, listed),
        [(nx * tall, depth)] * (1 + NT),
        in_specs=[VMEM, VMEM],
        scratch=[pltpu.VMEM((listed, wide), jnp.bfloat16), pltpu.VMEM((1, listed), jnp.int32)],
        flops=2 * nx * tall * listed * wide,
        moved=4 * (1 + NT) * nx * tall * depth,
    )(receiver_cells, observed)

    padded = pltpu.VMEM((nx + 2, tall + 16, depth), jnp.float32)
    plain = pltpu.VMEM((nx, tall, depth), jnp.float32)
    half = rows // 2
    *turned, keep, give = call(
        functools.partial(steps, blocks, planes, rows, depth, ny),
        [(planes * rows, depth)] * blocks + [(nx * half, depth)] * 2,
        in_specs=[SMEM, SMEM] + [VMEM] * (2 * blocks + 1 + NT),
        scratch=[padded] * (NT + 1) + [plain] * NT + [plain, padded, plain] + [plain] * 3 + [padded] * 2,
        flops=2 * NT * 20 * nx * tall * depth,
        moved=4 * 10 * nx * tall * depth,
    )(source_cell, wavelet, *early, *late, *heard)

    got = across(give, lambda shot, dom: (shot ^ 1, dom))
    pieces = call(functools.partial(cut, blocks), [(planes * half, depth)] * blocks, in_specs=[VMEM] * 2)(keep, got)
    pieces = over_dom(pieces)
    turned = over_dom(turned)
    pieces = call(
        functools.partial(sort, blocks),
        [(planes * half, depth)] * blocks,
        in_specs=[VMEM] * blocks,
        scratch=[pltpu.VMEM((blocks, planes * half, depth), jnp.float32)],
    )(*pieces)
    pieces = over_pairs(pieces)
    (wave_next,) = call(functools.partial(join, planes, rows), [(planes, ny, depth)], in_specs=[VMEM] * blocks)(*turned)
    (total,) = call(functools.partial(add, planes), [(planes, half, depth)], in_specs=[VMEM] * blocks)(*pieces)
    return total, wave_next[None]


def solution(mesh):
    return jax.shard_map(
        shards,
        mesh=mesh,
        in_specs=(
            P("dom", None, None),
            P("shot", "dom", None, None),
            P("shot", "dom", None, None),
            P("shot", None),
            P("shot"),
            P("shot", None),
            P("shot", None, None),
        ),
        out_specs=(P("dom", "shot", None), P("shot", "dom", None, None)),
        check_vma=False,
    )
```

```python
import functools

import jax
import jax.numpy as jnp
from jax import lax
from jax.experimental import pallas as pl
from jax.experimental.pallas import tpu as pltpu
from jax.sharding import PartitionSpec as P

NT = 4
PRIOR_GAIN = 50.0
EDGE = 8
VMEM = pl.BlockSpec(memory_space=pltpu.VMEM)
HBM = pl.BlockSpec(memory_space=pltpu.HBM)
SMEM = pl.BlockSpec(memory_space=pltpu.SMEM)
LIMIT = 48 * 1024 * 1024
BLOCK = 768


def stay(array):
    return pltpu.with_memory_space_constraint(array, pltpu.HBM)


def call(body, out_rows, scratch=(), in_specs=(), flops=0, moved=0):
    return pl.pallas_call(
        body,
        out_shape=[jax.ShapeDtypeStruct(*s) if isinstance(s[0], tuple) else jax.ShapeDtypeStruct(s, jnp.float32) for s in out_rows],
        in_specs=list(in_specs),
        out_specs=[VMEM] * len(out_rows),
        scratch_shapes=list(scratch),
        compiler_params=pltpu.CompilerParams(vmem_limit_bytes=LIMIT),
        cost_estimate=pl.CostEstimate(flops=flops, bytes_accessed=moved, transcendentals=0),
    )


def window(field, plane, block, blocks, rows):
    first = pl.multiple_of(block * rows, 8)
    above = pl.multiple_of(jnp.maximum(first - EDGE, 0), 8)
    below = pl.multiple_of(jnp.minimum(first + rows, (blocks * rows) - EDGE), 8)
    top = field[plane, pl.ds(above, EDGE), :]
    bottom = field[plane, pl.ds(below, EDGE), :]
    top = jnp.where(block > 0, top, 0.0)
    bottom = jnp.where(block < blocks - 1, bottom, 0.0)
    return top, field[plane, pl.ds(first, rows), :], bottom


def put(field, plane, block, blocks, rows, out, at):
    top, core, bottom = window(field, plane, block, blocks, rows)
    out[at : at + EDGE, :] = top
    out[at + EDGE : at + EDGE + rows, :] = core
    out[at + EDGE + rows : at + rows + 2 * EDGE, :] = bottom


def fetch(field, held, semaphores):
    copies = [pltpu.make_async_copy(field.at[p], held.at[p], semaphores.at[p]) for p in range(held.shape[0])]
    for copy in copies:
        copy.start()
    return copies


def pack_kappa(blocks, planes, rows, kappa, *refs):
    outs, (held, whole, semaphores) = refs[:blocks], refs[blocks:]
    copies = fetch(kappa, held, semaphores)
    dom = lax.axis_index("dom")
    core = lax.rem(lax.axis_index("shot"), 2)
    tall = rows + 2 * EDGE
    half = tall // 2
    for p in range(planes):
        copies[p].wait()
        put(held, p, dom, blocks, rows, outs[0], p * tall)
        for s in range(1, blocks):
            put(held, p, lax.bitwise_xor(dom, s), blocks, rows, whole, 0)
            outs[s][p * half : (p + 1) * half, :] = whole[pl.ds(pl.multiple_of(core * half, 8), half), :]


def pack_waves(blocks, planes, rows, now, before, *refs):
    outs, (held_now, held_before, semaphores) = refs[:blocks], refs[blocks:]
    fields = (held_now, held_before)
    copies = fetch(now, held_now, semaphores.at[0]) + fetch(before, held_before, semaphores.at[1])
    dom = lax.axis_index("dom")
    tall = rows + 2 * EDGE
    for f, field in enumerate(fields):
        for p in range(planes):
            copies[f * planes + p].wait()
            for s in range(blocks):
                put(field, p, lax.bitwise_xor(dom, s), blocks, rows, outs[s], (f * planes + p) * tall)


def gather(*refs):
    out = refs[-1]
    size = refs[0].shape[0]
    for i, ref in enumerate(refs[:-1]):
        out[i * size : (i + 1) * size, :] = ref[...]


def spread(depth, ny, rows, count, source, lists_at, cells_at, observed_at, *refs):
    count_ref, heard_ref, pulse_ref, listed, wavelet, cells_ref, observed_ref, semaphores = refs
    copies = [
        pltpu.make_async_copy(lists_at, wavelet, semaphores.at[0]),
        pltpu.make_async_copy(cells_at, cells_ref, semaphores.at[1]),
        pltpu.make_async_copy(observed_at, observed_ref, semaphores.at[2]),
    ]
    for copy in copies:
        copy.start()
    tall = rows + 2 * EDGE
    size = count_ref.shape[0]
    dom = lax.axis_index("dom")
    spot = lax.rem(source[0], depth)
    lane = lax.broadcasted_iota(jnp.int32, (1, depth), 1)
    count_ref[...] = jnp.zeros_like(count_ref)
    heard_ref[...] = jnp.zeros_like(heard_ref)
    for copy in copies:
        copy.wait()
    for n in range(NT):
        pulse_ref[n : n + 1, :] = jnp.where(lane == spot, wavelet[:, n : n + 1], 0.0)
    cells = cells_ref[...]
    line = cells // depth
    x = line // ny
    y = line - x * ny - (dom * rows - EDGE)
    here = (y >= 0) & (y < tall)
    row = x * tall + jnp.clip(y, 0, tall - 1)
    coarse = row // 64
    stack = [array.astype(jnp.float32) for array in (coarse, row - coarse * 64, cells - line * depth)]
    left = observed_ref[0]
    for part in range(3):
        piece = left.astype(jnp.bfloat16).astype(jnp.float32)
        left = left - piece
        stack.append(piece)
    stack = jnp.concatenate(stack + [jnp.zeros((13 - 3 * NT, count), jnp.float32)], axis=0)

    columns = 128
    ones = jnp.where(here, 1.0, 0.0)
    ones = jnp.concatenate([ones[:, j : j + columns] for j in range(0, count, columns)], axis=0)
    square = (columns, columns)
    down, across = lax.broadcasted_iota(jnp.int32, square, 0), lax.broadcasted_iota(jnp.int32, square, 1)
    order = jnp.dot(ones, jnp.where(down < across, 1.0, 0.0), preferred_element_type=jnp.float32)
    order = jnp.where(ones > 0.0, order, -1.0)
    slots = down.astype(jnp.float32)
    total = 0
    for j in range(count // columns):
        turned = stack[:, j * columns : (j + 1) * columns].T.astype(jnp.bfloat16)
        move = jnp.where(slots == order[j : j + 1, :], 1.0, 0.0).astype(jnp.bfloat16)
        listed[pl.ds(total, columns), 0:16] = jnp.dot(move, turned, preferred_element_type=jnp.float32)
        total = total + jnp.sum(ones[j : j + 1, :]).astype(jnp.int32)

    def block(k, _):
        first = pl.multiple_of(k * BLOCK, 8)
        which = lax.broadcasted_iota(jnp.int32, (BLOCK, 16), 0) + first
        some = jnp.where(which < total, listed[pl.ds(first, BLOCK), 0:16], -1.0)
        flat = some.T
        ids = (flat[0:1, :] * 64.0 + flat[1:2, :]).astype(jnp.int32)
        hot = jnp.where(lax.broadcasted_iota(jnp.int32, (size, BLOCK), 0) == ids, 1.0, 0.0).astype(jnp.bfloat16)
        at = lax.broadcasted_iota(jnp.int32, (BLOCK, depth), 1).astype(jnp.float32) == some[:, 2:3]
        at = jnp.where(at, 1.0, 0.0).astype(jnp.bfloat16)
        some = some.astype(jnp.bfloat16)
        value = [at] + [at * some[:, 3 + i : 4 + i] for i in range(3 * NT)]
        out = jnp.dot(hot, jnp.concatenate(value, axis=1), preferred_element_type=jnp.float32)
        count_ref[...] += out[:, 0:depth]
        for n in range(NT):
            high, mid, low = (out[:, i * depth : (i + 1) * depth] for i in (1 + n, 1 + NT + n, 1 + 2 * NT + n))
            heard_ref[n] += high + (mid + low)
        return 0

    lax.fori_loop(0, (total + BLOCK - 1) // BLOCK, block, 0)


def bend(field, at, first, some, nx, x, planes_held, low, high):
    under, mid, over = planes_held
    total = field[(*at, x, pl.ds(first + 1, some))] + field[(*at, x, pl.ds(first - 1, some))]
    up = jnp.where(high, 0.0, pltpu.roll(mid, mid.shape[1] - 1, 1))
    down = jnp.where(low, 0.0, pltpu.roll(mid, 1, 1))
    total = total + (up + down)
    if x > 0:
        total = total + under
    if x < nx - 1:
        total = total + over
    return total


def sweep(field, at, first, some, nx):
    under, mid = None, field[(*at, 0, pl.ds(first, some))]
    for x in range(nx):
        over = field[(*at, x + 1, pl.ds(first, some))] if x < nx - 1 else None
        yield x, (under, mid, over)
        under, mid = mid, over


def steps(blocks, planes, rows, depth, ny, *refs):
    source, pulse, count, heard, refs = *refs[:4], refs[4:]
    kappas, refs = refs[:blocks], refs[blocks:]
    others, waves, refs = refs[0], refs[1 : 1 + blocks], refs[1 + blocks :]
    turned, (keep, give) = refs[:blocks], refs[blocks : blocks + 2]
    wave, lap, model, image, adjoint, weighted = refs[blocks + 2 :]
    tall = rows + 2 * EDGE
    nx = blocks * planes
    dom = lax.axis_index("dom")
    shot = lax.axis_index("shot")
    core = lax.rem(shot, 2)
    body = pl.ds(8, tall)

    half = tall // 2
    near = pl.ds(pl.multiple_of(8 + core * half, 8), half)
    far = pl.ds(pl.multiple_of(8 + (1 - core) * half, 8), half)
    for s in range(blocks):
        first = planes * lax.bitwise_xor(dom, s)
        for p in range(planes):
            wave[1, first + p, body, :] = waves[s][p * tall : (p + 1) * tall, :]
            wave[0, first + p, body, :] = waves[s][(planes + p) * tall : (planes + p + 1) * tall, :]
            if s == 0:
                model[first + p, body, :] = kappas[s][p * tall : (p + 1) * tall, :]
            else:
                model[first + p, near, :] = kappas[s][p * half : (p + 1) * half, :]
                at = ((s - 1) * planes + p) * half
                model[first + p, far, :] = others[at : at + half, :]

    some = 48
    lanes = lax.broadcasted_iota(jnp.int32, (some, depth), 1)
    low, high = lanes == 0, lanes == depth - 1
    line = source[0] // depth
    sx = line // ny
    sy = line - sx * ny - (dom * rows - EDGE)
    source_here = (sy >= 0) & (sy < tall)
    sy = 8 + jnp.clip(sy, 0, tall - 1)

    def forward(n, _):
        for a in range(0, tall, some):
            rows_at = pl.ds(8 + a, some)
            for x, held in sweep(wave, (n + 1,), 8 + a, some, nx):
                mid = held[1]
                bent = bend(wave, (n + 1,), 8 + a, some, nx, x, held, low, high) - 6.0 * mid
                lap[n, x, a : a + some, :] = bent
                new = (mid + mid) - wave[n, x, rows_at, :] + model[x, rows_at, :] * bent
                wave[n + 2, x, rows_at, :] = new

        @pl.when(source_here)
        def _():
            wave[n + 2, sx, pl.ds(sy, 1), :] = wave[n + 2, sx, pl.ds(sy, 1), :] + pulse[pl.ds(n, 1), :]

        return 0

    lax.fori_loop(0, NT, forward, 0)

    for s in range(blocks):
        first = planes * lax.bitwise_xor(dom, s)
        for p in range(planes):
            turned[s][p * rows : (p + 1) * rows, :] = wave[NT + 1, first + p, 8 + EDGE : 8 + EDGE + rows, :]

    for a in range(0, tall, some):
        rows_at = pl.ds(8 + a, some)
        for x in range(nx):
            at = slice(x * tall + a, x * tall + a + some)
            now = count[at, :] * wave[NT + 1, x, rows_at, :] - heard[NT - 1, at, :]
            adjoint[NT % 2, x, a : a + some, :] = now
            adjoint[1 - NT % 2, x, a : a + some, :] = jnp.zeros_like(now)
            weighted[NT % 2, x, rows_at, :] = now * model[x, rows_at, :]
            image[x, a : a + some, :] = now * lap[NT - 1, x, a : a + some, :]

    def level_of(level, last):
        new, old = level % 2, 1 - level % 2
        for a in range(0, tall, some):
            rows_at = pl.ds(8 + a, some)
            for x, held in sweep(weighted, (old,), 8 + a, some, nx):
                at = slice(x * tall + a, x * tall + a + some)
                bent = bend(weighted, (old,), 8 + a, some, nx, x, held, low, high) - 6.0 * held[1]
                after = adjoint[old, x, a : a + some, :]
                now = count[at, :] * wave[level + 1, x, rows_at, :] - heard[level - 1, at, :]
                now = (now + bent) + ((after + after) - adjoint[new, x, a : a + some, :])
                part = image[x, a : a + some, :] + now * lap[level - 1, x, a : a + some, :]
                if not last:
                    adjoint[new, x, a : a + some, :] = now
                    weighted[new, x, rows_at, :] = now * model[x, rows_at, :]
                image[x, a : a + some, :] = part

    def backward(i, _):
        level_of(NT - 1 - i, False)
        return 0

    lax.fori_loop(0, NT - 2, backward, 0)
    level_of(1, True)

    half = rows // 2
    mine = pl.multiple_of(EDGE + core * half, 8)
    mates = pl.multiple_of(EDGE + (1 - core) * half, 8)

    @pl.when(shot == 0)
    def _():
        for a in range(0, tall, some):
            for x, held in sweep(model, (), 8 + a, some, nx):
                total = bend(model, (), 8 + a, some, nx, x, held, low, high)
                score = (total / 6.0 - held[1]) * (PRIOR_GAIN * NT)
                image[x, a : a + some, :] = image[x, a : a + some, :] - score

    for x in range(nx):
        keep[x * half : (x + 1) * half, :] = image[x, pl.ds(mine, half), :] / NT
        give[x * half : (x + 1) * half, :] = image[x, pl.ds(mates, half), :] / NT


def cut(blocks, keep, got, *outs):
    dom = lax.axis_index("dom")
    size = outs[0].shape[0]
    for s in range(blocks):
        at = pl.ds(pl.multiple_of(lax.bitwise_xor(dom, s) * size, 8), size)
        outs[s][...] = keep[at, :] + got[at, :]


def sort(blocks, *refs):
    came, outs, held = refs[:blocks], refs[blocks : 2 * blocks], refs[2 * blocks]
    dom, pair = lax.axis_index("dom"), lax.axis_index("shot") // 2
    for s in range(blocks):
        held[lax.bitwise_xor(dom, s)] = came[s][...]
    for s in range(blocks):
        outs[s][...] = held[lax.bitwise_xor(pair, s)]


def add(planes, *refs):
    out = refs[-1]
    size = out.shape[1]
    for p in range(planes):
        total = refs[0][p * size : (p + 1) * size, :]
        for ref in refs[1:-1]:
            total = total + ref[p * size : (p + 1) * size, :]
        out[p] = total


def join(planes, rows, *refs):
    out = refs[-1]
    dom = lax.axis_index("dom")
    for s, ref in enumerate(refs[:-1]):
        at = pl.ds(pl.multiple_of(lax.bitwise_xor(dom, s) * rows, 8), rows)
        for p in range(planes):
            out[p, at, :] = ref[p * rows : (p + 1) * rows, :]


def shards(kappa, wave_now, wave_before, wavelet, source_cell, receiver_cells, observed):
    shots, blocks = lax.axis_size("shot"), lax.axis_size("dom")
    _, planes, ny, depth = wave_now.shape
    rows = ny // blocks
    tall = rows + 2 * EDGE
    nx = planes * blocks
    listed = receiver_cells.shape[1]

    def across(array, to):
        pairs = []
        for shot in range(shots):
            for dom in range(blocks):
                there = to(shot, dom)
                pairs.append((shot * blocks + dom, there[0] * blocks + there[1]))
        return lax.ppermute(array, ("shot", "dom"), pairs)

    def over_dom(arrays):
        return [arrays[0]] + [across(arrays[s], lambda shot, dom, s=s: (shot, dom ^ s)) for s in range(1, blocks)]

    def over_pairs(arrays):
        return [arrays[0]] + [across(arrays[s], lambda shot, dom, s=s: (shot ^ (2 * s), dom)) for s in range(1, blocks)]

    half = tall // 2
    held = pltpu.VMEM((planes, ny, depth), jnp.float32)
    kappas = call(
        functools.partial(pack_kappa, blocks, planes, rows),
        [(planes * tall, depth)] + [(planes * half, depth)] * (blocks - 1),
        in_specs=[HBM],
        scratch=[held, pltpu.VMEM((tall, depth), jnp.float32), pltpu.SemaphoreType.DMA((planes,))],
    )(stay(kappa))
    waves = call(
        functools.partial(pack_waves, blocks, planes, rows),
        [(2 * planes * tall, depth)] * blocks,
        in_specs=[HBM] * 2,
        scratch=[held, held, pltpu.SemaphoreType.DMA((2, planes))],
    )(stay(wave_now[0]), stay(wave_before[0]))
    kappas = over_dom(kappas)
    waves = over_dom(waves)
    (gathered,) = call(gather, [((blocks - 1) * planes * half, depth)], in_specs=[VMEM] * (blocks - 1))(*kappas[1:])
    others = across(gathered, lambda shot, dom: (shot ^ 1, dom))

    wide = (1 + 3 * NT) * depth
    count, heard, pulse = call(
        functools.partial(spread, depth, ny, rows, listed),
        [(nx * tall, depth), (NT, nx * tall, depth), (NT, depth)],
        in_specs=[SMEM, HBM, HBM, HBM],
        scratch=[pltpu.VMEM((listed + BLOCK, depth), jnp.float32)]
        + [pltpu.VMEM(array.shape, array.dtype) for array in (wavelet, receiver_cells, observed)]
        + [pltpu.SemaphoreType.DMA((3,))],
        flops=2 * nx * tall * BLOCK * wide,
        moved=4 * (1 + NT) * nx * tall * depth,
    )(source_cell, stay(wavelet), stay(receiver_cells), stay(observed))

    half = rows // 2
    *turned, keep, give = call(
        functools.partial(steps, blocks, planes, rows, depth, ny),
        [(planes * rows, depth)] * blocks + [(nx * half, depth)] * 2,
        in_specs=[SMEM] + [VMEM] * (2 * blocks + 4),
        scratch=[
            pltpu.VMEM((NT + 2, nx, tall + 16, depth), jnp.float32),
            pltpu.VMEM((NT, nx, tall, depth), jnp.float32),
            pltpu.VMEM((nx, tall + 16, depth), jnp.float32),
            pltpu.VMEM((nx, tall, depth), jnp.float32),
            pltpu.VMEM((2, nx, tall, depth), jnp.float32),
            pltpu.VMEM((2, nx, tall + 16, depth), jnp.float32),
        ],
        flops=2 * NT * 20 * nx * tall * depth,
        moved=4 * 10 * nx * tall * depth,
    )(source_cell, pulse, count, heard, *kappas, others, *waves)

    got = across(give, lambda shot, dom: (shot ^ 1, dom))
    pieces = call(functools.partial(cut, blocks), [(planes * half, depth)] * blocks, in_specs=[VMEM] * 2)(keep, got)
    pieces = over_dom(pieces)
    turned = over_dom(turned)
    pieces = call(
        functools.partial(sort, blocks),
        [(planes * half, depth)] * blocks,
        in_specs=[VMEM] * blocks,
        scratch=[pltpu.VMEM((blocks, planes * half, depth), jnp.float32)],
    )(*pieces)
    pieces = over_pairs(pieces)
    (wave_next,) = call(functools.partial(join, planes, rows), [(planes, ny, depth)], in_specs=[VMEM] * blocks)(*turned)
    (total,) = call(functools.partial(add, planes), [(planes, half, depth)], in_specs=[VMEM] * blocks)(*pieces)
    return total, wave_next[None]


def solution(mesh):
    return jax.shard_map(
        shards,
        mesh=mesh,
        in_specs=(
            P("dom", None, None),
            P("shot", "dom", None, None),
            P("shot", "dom", None, None),
            P("shot", None),
            P("shot"),
            P("shot", None),
            P("shot", None, None),
        ),
        out_specs=(P("dom", "shot", None), P("shot", "dom", None, None)),
        check_vma=False,
    )
```

```python
import functools

import jax
import jax.numpy as jnp
from jax import lax
from jax.experimental import pallas as pl
from jax.experimental.pallas import tpu as pltpu
from jax.sharding import PartitionSpec as P

NT = 4
PRIOR_GAIN = 50.0
EDGE = 8
VMEM = pl.BlockSpec(memory_space=pltpu.VMEM)
HBM = pl.BlockSpec(memory_space=pltpu.HBM)
SMEM = pl.BlockSpec(memory_space=pltpu.SMEM)
LIMIT = 32 * 1024 * 1024
BLOCK = 768


def stay(array):
    return pltpu.with_memory_space_constraint(array, pltpu.HBM)


def call(body, out_rows, scratch=(), in_specs=(), flops=0, moved=0):
    return pl.pallas_call(
        body,
        out_shape=[jax.ShapeDtypeStruct(*s) if isinstance(s[0], tuple) else jax.ShapeDtypeStruct(s, jnp.float32) for s in out_rows],
        in_specs=list(in_specs),
        out_specs=[VMEM] * len(out_rows),
        scratch_shapes=list(scratch),
        compiler_params=pltpu.CompilerParams(vmem_limit_bytes=LIMIT),
        cost_estimate=pl.CostEstimate(flops=flops, bytes_accessed=moved, transcendentals=0),
    )


def window(field, plane, block, blocks, rows):
    first = pl.multiple_of(block * rows, 8)
    above = pl.multiple_of(jnp.maximum(first - EDGE, 0), 8)
    below = pl.multiple_of(jnp.minimum(first + rows, (blocks * rows) - EDGE), 8)
    top = field[plane, pl.ds(above, EDGE), :]
    bottom = field[plane, pl.ds(below, EDGE), :]
    top = jnp.where(block > 0, top, 0.0)
    bottom = jnp.where(block < blocks - 1, bottom, 0.0)
    return top, field[plane, pl.ds(first, rows), :], bottom


def put(field, plane, block, blocks, rows, out, at):
    top, core, bottom = window(field, plane, block, blocks, rows)
    out[at : at + EDGE, :] = top
    out[at + EDGE : at + EDGE + rows, :] = core
    out[at + EDGE + rows : at + rows + 2 * EDGE, :] = bottom


def fetch(field, held, semaphores):
    copies = [pltpu.make_async_copy(field.at[p], held.at[p], semaphores.at[p]) for p in range(held.shape[0])]
    for copy in copies:
        copy.start()
    return copies


def pack_early(blocks, planes, rows, kappa, now, *refs):
    outs, (held, model, whole, semaphores) = refs[: blocks - 1], refs[blocks - 1 :]
    dom, core = lax.axis_index("dom"), lax.rem(lax.axis_index("shot"), 2)
    copies = [pltpu.make_async_copy(now.at[0], held.at[0], semaphores.at[planes])]
    copies[0].start()
    copies += fetch(kappa, model, semaphores)
    tall = rows + 2 * EDGE
    half = tall // 2
    copies[0].wait()
    for s in range(1, blocks):
        put(held, 0, lax.bitwise_xor(dom, s), blocks, rows, outs[s - 1], 0)
    for p in range(planes):
        copies[1 + p].wait()
        for s in range(1, blocks):
            put(model, p, lax.bitwise_xor(dom, s), blocks, rows, whole, 0)
            at = tall + p * half
            outs[s - 1][at : at + half, :] = whole[pl.ds(pl.multiple_of(core * half, 8), half), :]


def pack_late(blocks, planes, rows, kappa, now, before, *refs):
    outs, own, refs = refs[: blocks - 1], refs[blocks - 1], refs[blocks:]
    held, semaphores = refs[:3], refs[3]
    fields = (now, before, kappa)
    copies = [fetch(field, ref, semaphores.at[i]) for i, (field, ref) in enumerate(zip(fields, held))]
    dom = lax.axis_index("dom")
    tall = rows + 2 * EDGE
    for f in range(3):
        for p in range(planes):
            copies[f][p].wait()
            put(held[f], p, dom, blocks, rows, own, (f * planes + p) * tall)
            to = f * planes + p - 1
            if f < 2 and to >= 0:
                for s in range(1, blocks):
                    put(held[f], p, lax.bitwise_xor(dom, s), blocks, rows, outs[s - 1], to * tall)


def gather(planes, half, *refs):
    parts, outs = refs[:-planes], refs[-planes:]
    for i, part in enumerate(parts):
        first = part.shape[0] - planes * half
        for p, out in enumerate(outs):
            out[i * half : (i + 1) * half, :] = part[first + p * half : first + (p + 1) * half, :]


def spread(depth, ny, rows, count, source, lists_at, cells_at, observed_at, *refs):
    count_ref, heard_ref, pulse_ref, listed, wavelet, cells_ref, observed_ref, semaphores = refs
    copies = [
        pltpu.make_async_copy(lists_at, wavelet, semaphores.at[0]),
        pltpu.make_async_copy(cells_at, cells_ref, semaphores.at[1]),
        pltpu.make_async_copy(observed_at, observed_ref, semaphores.at[2]),
    ]
    for copy in copies:
        copy.start()
    tall = rows + 2 * EDGE
    size = count_ref.shape[0]
    dom = lax.axis_index("dom")
    spot = lax.rem(source[0], depth)
    lane = lax.broadcasted_iota(jnp.int32, (1, depth), 1)
    count_ref[...] = jnp.zeros_like(count_ref)
    heard_ref[...] = jnp.zeros_like(heard_ref)
    for copy in copies:
        copy.wait()
    for n in range(NT):
        pulse_ref[n : n + 1, :] = jnp.where(lane == spot, wavelet[:, n : n + 1], 0.0)
    cells = cells_ref[...]
    line = cells // depth
    x = line // ny
    y = line - x * ny - (dom * rows - EDGE)
    here = (y >= 0) & (y < tall)
    row = x * tall + jnp.clip(y, 0, tall - 1)
    coarse = row // 64
    stack = [array.astype(jnp.float32) for array in (coarse, row - coarse * 64, cells - line * depth)]
    left = observed_ref[0]
    for part in range(3):
        piece = left.astype(jnp.bfloat16).astype(jnp.float32)
        left = left - piece
        stack.append(piece)
    stack = jnp.concatenate(stack + [jnp.zeros((13 - 3 * NT, count), jnp.float32)], axis=0)

    columns = 128
    ones = jnp.where(here, 1.0, 0.0)
    ones = jnp.concatenate([ones[:, j : j + columns] for j in range(0, count, columns)], axis=0)
    square = (columns, columns)
    down, across = lax.broadcasted_iota(jnp.int32, square, 0), lax.broadcasted_iota(jnp.int32, square, 1)
    order = jnp.dot(ones, jnp.where(down < across, 1.0, 0.0), preferred_element_type=jnp.float32)
    order = jnp.where(ones > 0.0, order, -1.0)
    slots = down.astype(jnp.float32)
    total = 0
    for j in range(count // columns):
        turned = stack[:, j * columns : (j + 1) * columns].T.astype(jnp.bfloat16)
        move = jnp.where(slots == order[j : j + 1, :], 1.0, 0.0).astype(jnp.bfloat16)
        listed[pl.ds(total, columns), 0:16] = jnp.dot(move, turned, preferred_element_type=jnp.float32)
        total = total + jnp.sum(ones[j : j + 1, :]).astype(jnp.int32)

    def block(k, _):
        first = pl.multiple_of(k * BLOCK, 8)
        which = lax.broadcasted_iota(jnp.int32, (BLOCK, 16), 0) + first
        some = jnp.where(which < total, listed[pl.ds(first, BLOCK), 0:16], -1.0)
        flat = some.T
        ids = (flat[0:1, :] * 64.0 + flat[1:2, :]).astype(jnp.int32)
        hot = jnp.where(lax.broadcasted_iota(jnp.int32, (size, BLOCK), 0) == ids, 1.0, 0.0).astype(jnp.bfloat16)
        at = lax.broadcasted_iota(jnp.int32, (BLOCK, depth), 1).astype(jnp.float32) == some[:, 2:3]
        at = jnp.where(at, 1.0, 0.0).astype(jnp.bfloat16)
        some = some.astype(jnp.bfloat16)
        value = [at] + [at * some[:, 3 + i : 4 + i] for i in range(3 * NT)]
        out = jnp.dot(hot, jnp.concatenate(value, axis=1), preferred_element_type=jnp.float32)
        count_ref[...] += out[:, 0:depth]
        for n in range(NT):
            high, mid, low = (out[:, i * depth : (i + 1) * depth] for i in (1 + n, 1 + NT + n, 1 + 2 * NT + n))
            heard_ref[n] += high + (mid + low)
        return 0

    lax.fori_loop(0, (total + BLOCK - 1) // BLOCK, block, 0)


def bend(field, at, first, some, nx, x, planes_held, low, high):
    under, mid, over = planes_held
    total = field[(*at, x, pl.ds(first + 1, some))] + field[(*at, x, pl.ds(first - 1, some))]
    up = jnp.where(high, 0.0, pltpu.roll(mid, mid.shape[1] - 1, 1))
    down = jnp.where(low, 0.0, pltpu.roll(mid, 1, 1))
    total = total + (up + down)
    if x > 0:
        total = total + under
    if x < nx - 1:
        total = total + over
    return total


def sweep(field, at, first, some, nx):
    under, mid = None, field[(*at, 0, pl.ds(first, some))]
    for x in range(nx):
        over = field[(*at, x + 1, pl.ds(first, some))] if x < nx - 1 else None
        yield x, (under, mid, over)
        under, mid = mid, over


def edges(some, depth):
    lanes = lax.broadcasted_iota(jnp.int32, (some, depth), 1)
    return lanes == 0, lanes == depth - 1


def forward(blocks, planes, rows, ny, source, pulse, *refs):
    early, late, own, refs = refs[: blocks - 1], refs[blocks - 1 : 2 * blocks - 2], refs[2 * blocks - 2], refs[2 * blocks - 1 :]
    swapped, refs = refs[:planes], refs[planes:]
    wave, lap, model, turned, start = *refs[:3], refs[3:-1], refs[-1]
    nx, tall, depth = lap.shape[1:]
    dom, core = lax.axis_index("dom"), lax.rem(lax.axis_index("shot"), 2)
    half = tall // 2
    near = pl.ds(pl.multiple_of(8 + core * half, 8), half)
    other = pl.ds(pl.multiple_of(8 + (1 - core) * half, 8), half)
    body = slice(8, 8 + tall)
    for s in range(blocks):
        first = planes * lax.bitwise_xor(dom, s)
        for p in range(planes):
            if s == 0:
                for f, to in enumerate((start.at[0], start.at[1], model)):
                    at = (f * planes + p) * tall
                    to[first + p, body, :] = own[at : at + tall, :]
                continue
            for f in range(2):
                i = f * planes + p - 1
                part = late[s - 1][i * tall : (i + 1) * tall, :] if i >= 0 else early[s - 1][0:tall, :]
                start[f, first + p, body, :] = part
            at = tall + p * half
            model[first + p, near, :] = early[s - 1][at : at + half, :]
            model[first + p, other, :] = swapped[p][(s - 1) * half : s * half, :]

    some = 48
    low, high = edges(some, depth)
    line = source[0] // depth
    sx = line // ny
    sy = line - sx * ny - (dom * rows - EDGE)
    source_here = (sy >= 0) & (sy < tall)
    sy = 8 + jnp.clip(sy, 0, tall - 1)

    def inject(n):
        @pl.when(source_here)
        def _():
            wave[n, sx, pl.ds(sy, 1), :] = wave[n, sx, pl.ds(sy, 1), :] + pulse[n : n + 1, :]

    for n in range(NT):
        source_of = (wave, (n - 1,)) if n > 0 else (start, (0,))
        older = (wave, n - 2) if n > 1 else (start, 1 - n)
        for a in range(0, tall, some):
            rows_at = slice(8 + a, 8 + a + some)
            for x, held in sweep(*source_of, 8 + a, some, nx):
                mid = held[1]
                turn = bend(*source_of, 8 + a, some, nx, x, held, low, high) - 6.0 * mid
                lap[n, x, a : a + some, :] = turn
                old = older[0][older[1], x, rows_at, :]
                wave[n, x, rows_at, :] = (mid + mid) - old + model[x, rows_at, :] * turn
        inject(n)

    for s in range(blocks):
        first = planes * lax.bitwise_xor(dom, s)
        for p in range(planes):
            turned[s][p * rows : (p + 1) * rows, :] = wave[NT - 1, first + p, 8 + EDGE : 8 + EDGE + rows, :]


def backward(mine, rows, count, heard, wave, lap, model, image, adjoint, weighted, gain):
    nx, tall, depth = lap.shape[1:]
    shot = lax.axis_index("shot")
    core = lax.rem(shot, 2)
    half = rows // 2
    wide = half + 2 * EDGE
    first = pl.multiple_of((core if mine else 1 - core) * half, 8)
    some = 40 if wide % 40 == 0 else 16
    low, high = edges(some, depth)

    def at(a, size=some, off=0):
        return pl.ds(pl.multiple_of(first + (a + off), 8), size)

    for a in range(0, wide, some):
        here = slice(a, a + some)
        for x in range(nx):
            now = count[at(a, off=x * tall), :] * wave[NT - 1, x, at(a, off=8), :] - heard[NT - 1, at(a, off=x * tall), :]
            adjoint[NT % 2, x, here, :] = now
            weighted[NT % 2, x, 8 + a : 8 + a + some, :] = now * model[x, at(a, off=8), :]
            gain[x, here, :] = now * lap[NT - 1, x, at(a), :]

    for level in range(NT - 1, 1, -1):
        new, old = level % 2, 1 - level % 2
        for a in range(0, wide, some):
            here = slice(a, a + some)
            for x, held in sweep(weighted, (old,), 8 + a, some, nx):
                turn = bend(weighted, (old,), 8 + a, some, nx, x, held, low, high) - 6.0 * held[1]
                after = adjoint[old, x, here, :]
                now = count[at(a, off=x * tall), :] * wave[level - 1, x, at(a, off=8), :]
                now = (now - heard[level - 1, at(a, off=x * tall), :]) + (turn + (after + after))
                if level < NT - 1:
                    now = now - adjoint[new, x, here, :]
                adjoint[new, x, here, :] = now
                weighted[new, x, 8 + a : 8 + a + some, :] = now * model[x, at(a, off=8), :]
                gain[x, here, :] = gain[x, here, :] + now * lap[level - 1, x, at(a), :]

    some = 32 if half % 32 == 0 else 16
    low, high = edges(some, depth)
    for a in range(EDGE, EDGE + half, some):
        here = slice(a, a + some)
        for x, held in sweep(weighted, (0,), 8 + a, some, nx):
            turn = bend(weighted, (0,), 8 + a, some, nx, x, held, low, high) - 6.0 * held[1]
            after = adjoint[0, x, here, :]
            now = count[at(a, some, x * tall), :] * wave[0, x, at(a, some, 8), :]
            now = (now - heard[0, at(a, some, x * tall), :]) + (turn + (after + after)) - adjoint[1, x, here, :]
            total = gain[x, here, :] + now * lap[0, x, at(a, some), :]
            image[x * half + a - EDGE : x * half + a - EDGE + some, :] = total / NT

    @pl.when(shot == 0)
    def _():
        for x in range(nx):
            weighted[0, x, 0 : wide + 16, :] = model[x, pl.ds(first, wide + 16), :]
        for a in range(EDGE, EDGE + half, some):
            for x, held in sweep(weighted, (0,), 8 + a, some, nx):
                total = bend(weighted, (0,), 8 + a, some, nx, x, held, low, high)
                score = (total / 6.0 - held[1]) * PRIOR_GAIN
                to = slice(x * half + a - EDGE, x * half + a - EDGE + some)
                image[to, :] = image[to, :] - score


def cut(blocks, keep, got, *outs):
    dom = lax.axis_index("dom")
    size = outs[0].shape[0]
    for s in range(blocks):
        at = pl.ds(pl.multiple_of(lax.bitwise_xor(dom, s) * size, 8), size)
        outs[s][...] = keep[at, :] + got[at, :]


def sort(blocks, *refs):
    came, outs, held = refs[:blocks], refs[blocks : 2 * blocks], refs[2 * blocks]
    dom, pair = lax.axis_index("dom"), lax.axis_index("shot") // 2
    for s in range(blocks):
        held[lax.bitwise_xor(dom, s)] = came[s][...]
    for s in range(blocks):
        outs[s][...] = held[lax.bitwise_xor(pair, s)]


def add(planes, *refs):
    out = refs[-1]
    size = out.shape[1]
    for p in range(planes):
        total = refs[0][p * size : (p + 1) * size, :]
        for ref in refs[1:-1]:
            total = total + ref[p * size : (p + 1) * size, :]
        out[p] = total


def join(planes, rows, *refs):
    out = refs[-1]
    dom = lax.axis_index("dom")
    for s, ref in enumerate(refs[:-1]):
        at = pl.ds(pl.multiple_of(lax.bitwise_xor(dom, s) * rows, 8), rows)
        for p in range(planes):
            out[p, at, :] = ref[p * rows : (p + 1) * rows, :]


def shards(kappa, wave_now, wave_before, wavelet, source_cell, receiver_cells, observed):
    shots, blocks = lax.axis_size("shot"), lax.axis_size("dom")
    _, planes, ny, depth = wave_now.shape
    rows = ny // blocks
    tall = rows + 2 * EDGE
    nx = planes * blocks
    listed = receiver_cells.shape[1]

    def across(array, to):
        pairs = []
        for shot in range(shots):
            for dom in range(blocks):
                there = to(shot, dom)
                pairs.append((shot * blocks + dom, there[0] * blocks + there[1]))
        return lax.ppermute(array, ("shot", "dom"), pairs)

    def over_dom(arrays):
        return [arrays[0]] + [across(arrays[s], lambda shot, dom, s=s: (shot, dom ^ s)) for s in range(1, blocks)]

    def over_pairs(arrays):
        return [arrays[0]] + [across(arrays[s], lambda shot, dom, s=s: (shot ^ (2 * s), dom)) for s in range(1, blocks)]

    half = tall // 2
    held = pltpu.VMEM((planes, ny, depth), jnp.float32)
    early = call(
        functools.partial(pack_early, blocks, planes, rows),
        [(tall + planes * half, depth)] * (blocks - 1),
        in_specs=[HBM] * 2,
        scratch=[
            pltpu.VMEM((1, ny, depth), jnp.float32),
            held,
            pltpu.VMEM((tall, depth), jnp.float32),
            pltpu.SemaphoreType.DMA((planes + 1,)),
        ],
    )(stay(kappa), stay(wave_now[0]))
    early, before = lax.optimization_barrier((early, wave_before[0]))
    *late, own = call(
        functools.partial(pack_late, blocks, planes, rows),
        [((2 * planes - 1) * tall, depth)] * (blocks - 1) + [(3 * planes * tall, depth)],
        in_specs=[HBM] * 3,
        scratch=[held, held, held, pltpu.SemaphoreType.DMA((3, planes))],
    )(stay(kappa), stay(wave_now[0]), stay(before))
    early = over_dom([None, *early])[1:]
    late = over_dom([None, *late])[1:]

    wide = (1 + 3 * NT) * depth
    count, heard, pulse = call(
        functools.partial(spread, depth, ny, rows, listed),
        [(nx * tall, depth), (NT, nx * tall, depth), (NT, depth)],
        in_specs=[SMEM, HBM, HBM, HBM],
        scratch=[pltpu.VMEM((listed + BLOCK, depth), jnp.float32)]
        + [pltpu.VMEM(array.shape, array.dtype) for array in (wavelet, receiver_cells, observed)]
        + [pltpu.SemaphoreType.DMA((3,))],
        flops=1000 * 1000 * 1000,
        moved=1,
    )(source_cell, stay(wavelet), stay(receiver_cells), stay(observed))

    came, pulse = lax.optimization_barrier((early, pulse))
    parts = call(
        functools.partial(gather, planes, half), [((blocks - 1) * half, depth)] * planes, in_specs=[VMEM] * (blocks - 1)
    )(*came)
    swapped = [across(part, lambda shot, dom: (shot ^ 1, dom)) for part in parts]

    padded, plain = (nx, tall + 16, depth), (nx, tall, depth)
    cells = nx * tall * depth
    wave, lap, model, *turned = call(
        functools.partial(forward, blocks, planes, rows, ny),
        [(NT, *padded), (NT, *plain), padded] + [(planes * rows, depth)] * blocks,
        in_specs=[SMEM] + [VMEM] * (2 * blocks + planes),
        scratch=[pltpu.VMEM((2, *padded), jnp.float32)],
        flops=16 * NT * cells,
        moved=16 * NT * cells,
    )(source_cell, pulse, *early, *late, own, *swapped)
    half = rows // 2
    side = half + 2 * EDGE
    give, keep = (
        call(
            functools.partial(backward, mine, rows),
            [(nx * half, depth)],
            in_specs=[VMEM] * 5,
            scratch=[
                pltpu.VMEM((2, nx, side, depth), jnp.float32),
                pltpu.VMEM((2, nx, side + 16, depth), jnp.float32),
                pltpu.VMEM((nx, side, depth), jnp.float32),
            ],
            flops=12 * NT * cells,
            moved=12 * NT * cells,
        )(count, heard, wave, lap, model)[0]
        for mine in (False, True)
    )

    got = across(give, lambda shot, dom: (shot ^ 1, dom))
    pieces = call(functools.partial(cut, blocks), [(planes * half, depth)] * blocks, in_specs=[VMEM] * 2)(keep, got)
    pieces = over_dom(pieces)
    turned = over_dom(turned)
    pieces = call(
        functools.partial(sort, blocks),
        [(planes * half, depth)] * blocks,
        in_specs=[VMEM] * blocks,
        scratch=[pltpu.VMEM((blocks, planes * half, depth), jnp.float32)],
        flops=1400 * 1000 * 1000,
        moved=1,
    )(*pieces)
    pieces = over_pairs(pieces)
    (wave_next,) = call(functools.partial(join, planes, rows), [(planes, ny, depth)], in_specs=[VMEM] * blocks)(*turned)
    (total,) = call(functools.partial(add, planes), [(planes, half, depth)], in_specs=[VMEM] * blocks)(*pieces)
    return total, wave_next[None]


def solution(mesh):
    return jax.shard_map(
        shards,
        mesh=mesh,
        in_specs=(
            P("dom", None, None),
            P("shot", "dom", None, None),
            P("shot", "dom", None, None),
            P("shot", None),
            P("shot"),
            P("shot", None),
            P("shot", None, None),
        ),
        out_specs=(P("dom", "shot", None), P("shot", "dom", None, None)),
        check_vma=False,
    )
```

```python
import functools

import jax
import jax.numpy as jnp
from jax import lax
from jax.experimental import pallas as pl
from jax.experimental.pallas import tpu as pltpu
from jax.sharding import PartitionSpec as P

NT = 4
PRIOR_GAIN = 50.0
EDGE = 8
VMEM = pl.BlockSpec(memory_space=pltpu.VMEM)
HBM = pl.BlockSpec(memory_space=pltpu.HBM)
SMEM = pl.BlockSpec(memory_space=pltpu.SMEM)
LIMIT = 32 * 1024 * 1024
BLOCK = 768


def stay(array):
    return pltpu.with_memory_space_constraint(array, pltpu.HBM)


def call(body, out_rows, scratch=(), in_specs=(), flops=0, moved=0):
    return pl.pallas_call(
        body,
        out_shape=[jax.ShapeDtypeStruct(*s) if isinstance(s[0], tuple) else jax.ShapeDtypeStruct(s, jnp.float32) for s in out_rows],
        in_specs=list(in_specs),
        out_specs=[VMEM] * len(out_rows),
        scratch_shapes=list(scratch),
        compiler_params=pltpu.CompilerParams(vmem_limit_bytes=LIMIT),
        cost_estimate=pl.CostEstimate(flops=flops, bytes_accessed=moved, transcendentals=0),
    )


def window(field, plane, block, blocks, rows):
    first = pl.multiple_of(block * rows, 8)
    above = pl.multiple_of(jnp.maximum(first - EDGE, 0), 8)
    below = pl.multiple_of(jnp.minimum(first + rows, (blocks * rows) - EDGE), 8)
    top = field[plane, pl.ds(above, EDGE), :]
    bottom = field[plane, pl.ds(below, EDGE), :]
    top = jnp.where(block > 0, top, 0.0)
    bottom = jnp.where(block < blocks - 1, bottom, 0.0)
    return top, field[plane, pl.ds(first, rows), :], bottom


def put(field, plane, block, blocks, rows, out, at):
    top, core, bottom = window(field, plane, block, blocks, rows)
    out[at : at + EDGE, :] = top
    out[at + EDGE : at + EDGE + rows, :] = core
    out[at + EDGE + rows : at + rows + 2 * EDGE, :] = bottom


def fetch(field, held, semaphores):
    copies = [pltpu.make_async_copy(field.at[p], held.at[p], semaphores.at[p]) for p in range(held.shape[0])]
    for copy in copies:
        copy.start()
    return copies


def pack_early(blocks, planes, rows, kappa, now, *refs):
    outs, (held, model, whole, semaphores) = refs[: blocks - 1], refs[blocks - 1 :]
    dom, core = lax.axis_index("dom"), lax.rem(lax.axis_index("shot"), 2)
    copies = [pltpu.make_async_copy(now.at[0], held.at[0], semaphores.at[planes])]
    copies[0].start()
    copies += fetch(kappa, model, semaphores)
    tall = rows + 2 * EDGE
    half = tall // 2
    copies[0].wait()
    for s in range(1, blocks):
        put(held, 0, lax.bitwise_xor(dom, s), blocks, rows, outs[s - 1], 0)
    for p in range(planes):
        copies[1 + p].wait()
        for s in range(1, blocks):
            put(model, p, lax.bitwise_xor(dom, s), blocks, rows, whole, 0)
            at = tall + p * half
            outs[s - 1][at : at + half, :] = whole[pl.ds(pl.multiple_of(core * half, 8), half), :]


def pack_late(blocks, planes, rows, kappa, now, before, *refs):
    outs, own, refs = refs[: blocks - 1], refs[blocks - 1], refs[blocks:]
    held, semaphores = refs[:3], refs[3]
    fields = (now, before, kappa)
    copies = [fetch(field, ref, semaphores.at[i]) for i, (field, ref) in enumerate(zip(fields, held))]
    dom = lax.axis_index("dom")
    tall = rows + 2 * EDGE
    for f in range(3):
        for p in range(planes):
            copies[f][p].wait()
            put(held[f], p, dom, blocks, rows, own, (f * planes + p) * tall)
            to = f * planes + p - 1
            if f < 2 and to >= 0:
                for s in range(1, blocks):
                    put(held[f], p, lax.bitwise_xor(dom, s), blocks, rows, outs[s - 1], to * tall)


def gather(planes, half, *refs):
    parts, outs = refs[:-planes], refs[-planes:]
    for i, part in enumerate(parts):
        first = part.shape[0] - planes * half
        for p, out in enumerate(outs):
            out[i * half : (i + 1) * half, :] = part[first + p * half : first + (p + 1) * half, :]


def spread(depth, ny, rows, count, source, lists_at, cells_at, observed_at, *refs):
    count_ref, heard_ref, pulse_ref, listed, wavelet, cells_ref, observed_ref, semaphores = refs
    copies = [
        pltpu.make_async_copy(lists_at, wavelet, semaphores.at[0]),
        pltpu.make_async_copy(cells_at, cells_ref, semaphores.at[1]),
        pltpu.make_async_copy(observed_at, observed_ref, semaphores.at[2]),
    ]
    for copy in copies:
        copy.start()
    tall = rows + 2 * EDGE
    size = count_ref.shape[0]
    dom = lax.axis_index("dom")
    spot = lax.rem(source[0], depth)
    lane = lax.broadcasted_iota(jnp.int32, (1, depth), 1)
    count_ref[...] = jnp.zeros_like(count_ref)
    heard_ref[...] = jnp.zeros_like(heard_ref)
    for copy in copies:
        copy.wait()
    for n in range(NT):
        pulse_ref[n : n + 1, :] = jnp.where(lane == spot, wavelet[:, n : n + 1], 0.0)
    cells = cells_ref[...]
    line = cells // depth
    x = line // ny
    y = line - x * ny - (dom * rows - EDGE)
    here = (y >= 0) & (y < tall)
    row = x * tall + jnp.clip(y, 0, tall - 1)
    coarse = row // 64
    stack = [array.astype(jnp.float32) for array in (coarse, row - coarse * 64, cells - line * depth)]
    left = observed_ref[0]
    for part in range(3):
        piece = left.astype(jnp.bfloat16).astype(jnp.float32)
        left = left - piece
        stack.append(piece)
    stack = jnp.concatenate(stack + [jnp.zeros((13 - 3 * NT, count), jnp.float32)], axis=0)

    columns = 128
    ones = jnp.where(here, 1.0, 0.0)
    ones = jnp.concatenate([ones[:, j : j + columns] for j in range(0, count, columns)], axis=0)
    square = (columns, columns)
    down, across = lax.broadcasted_iota(jnp.int32, square, 0), lax.broadcasted_iota(jnp.int32, square, 1)
    order = jnp.dot(ones, jnp.where(down < across, 1.0, 0.0), preferred_element_type=jnp.float32)
    order = jnp.where(ones > 0.0, order, -1.0)
    slots = down.astype(jnp.float32)
    total = 0
    for j in range(count // columns):
        turned = stack[:, j * columns : (j + 1) * columns].T.astype(jnp.bfloat16)
        move = jnp.where(slots == order[j : j + 1, :], 1.0, 0.0).astype(jnp.bfloat16)
        listed[pl.ds(total, columns), 0:16] = jnp.dot(move, turned, preferred_element_type=jnp.float32)
        total = total + jnp.sum(ones[j : j + 1, :]).astype(jnp.int32)

    def block(k, _):
        first = pl.multiple_of(k * BLOCK, 8)
        which = lax.broadcasted_iota(jnp.int32, (BLOCK, 16), 0) + first
        some = jnp.where(which < total, listed[pl.ds(first, BLOCK), 0:16], -1.0)
        flat = some.T
        ids = (flat[0:1, :] * 64.0 + flat[1:2, :]).astype(jnp.int32)
        hot = jnp.where(lax.broadcasted_iota(jnp.int32, (size, BLOCK), 0) == ids, 1.0, 0.0).astype(jnp.bfloat16)
        at = lax.broadcasted_iota(jnp.int32, (BLOCK, depth), 1).astype(jnp.float32) == some[:, 2:3]
        at = jnp.where(at, 1.0, 0.0).astype(jnp.bfloat16)
        some = some.astype(jnp.bfloat16)
        value = [at] + [at * some[:, 3 + i : 4 + i] for i in range(3 * NT)]
        out = jnp.dot(hot, jnp.concatenate(value, axis=1), preferred_element_type=jnp.float32)
        count_ref[...] += out[:, 0:depth]
        for n in range(NT):
            high, mid, low = (out[:, i * depth : (i + 1) * depth] for i in (1 + n, 1 + NT + n, 1 + 2 * NT + n))
            heard_ref[n] += high + (mid + low)
        return 0

    lax.fori_loop(0, (total + BLOCK - 1) // BLOCK, block, 0)


def bend(field, at, first, some, nx, x, planes_held, low, high):
    under, mid, over = planes_held
    total = field[(*at, x, pl.ds(first + 1, some))] + field[(*at, x, pl.ds(first - 1, some))]
    up = jnp.where(high, 0.0, pltpu.roll(mid, mid.shape[1] - 1, 1))
    down = jnp.where(low, 0.0, pltpu.roll(mid, 1, 1))
    total = total + (up + down)
    if x > 0:
        total = total + under
    if x < nx - 1:
        total = total + over
    return total


def sweep(field, at, first, some, nx):
    under, mid = None, field[(*at, 0, pl.ds(first, some))]
    for x in range(nx):
        over = field[(*at, x + 1, pl.ds(first, some))] if x < nx - 1 else None
        yield x, (under, mid, over)
        under, mid = mid, over


def edges(some, depth):
    lanes = lax.broadcasted_iota(jnp.int32, (some, depth), 1)
    return lanes == 0, lanes == depth - 1


def forward(blocks, planes, rows, ny, source, pulse, *refs):
    early, late, own, refs = refs[: blocks - 1], refs[blocks - 1 : 2 * blocks - 2], refs[2 * blocks - 2], refs[2 * blocks - 1 :]
    swapped, refs = refs[:planes], refs[planes:]
    wave, lap, model, turned, start = *refs[:3], refs[3:-1], refs[-1]
    nx, tall, depth = lap.shape[1:]
    dom, core = lax.axis_index("dom"), lax.rem(lax.axis_index("shot"), 2)
    half = tall // 2
    near = pl.ds(pl.multiple_of(8 + core * half, 8), half)
    other = pl.ds(pl.multiple_of(8 + (1 - core) * half, 8), half)
    body = slice(8, 8 + tall)
    for s in range(blocks):
        first = planes * lax.bitwise_xor(dom, s)
        for p in range(planes):
            if s == 0:
                for f, to in enumerate((start.at[0], start.at[1], model)):
                    at = (f * planes + p) * tall
                    to[first + p, body, :] = own[at : at + tall, :]
                continue
            for f in range(2):
                i = f * planes + p - 1
                part = late[s - 1][i * tall : (i + 1) * tall, :] if i >= 0 else early[s - 1][0:tall, :]
                start[f, first + p, body, :] = part
            at = tall + p * half
            model[first + p, near, :] = early[s - 1][at : at + half, :]
            model[first + p, other, :] = swapped[p][(s - 1) * half : s * half, :]

    some = 48
    low, high = edges(some, depth)
    line = source[0] // depth
    sx = line // ny
    sy = line - sx * ny - (dom * rows - EDGE)
    source_here = (sy >= 0) & (sy < tall)
    sy = 8 + jnp.clip(sy, 0, tall - 1)

    def inject(n):
        @pl.when(source_here)
        def _():
            wave[n, sx, pl.ds(sy, 1), :] = wave[n, sx, pl.ds(sy, 1), :] + pulse[n : n + 1, :]

    for n in range(NT):
        source_of = (wave, (n - 1,)) if n > 0 else (start, (0,))
        older = (wave, n - 2) if n > 1 else (start, 1 - n)
        for a in range(0, tall, some):
            rows_at = slice(8 + a, 8 + a + some)
            for x, held in sweep(*source_of, 8 + a, some, nx):
                mid = held[1]
                turn = bend(*source_of, 8 + a, some, nx, x, held, low, high) - 6.0 * mid
                lap[n, x, a : a + some, :] = turn
                old = older[0][older[1], x, rows_at, :]
                wave[n, x, rows_at, :] = (mid + mid) - old + model[x, rows_at, :] * turn
        inject(n)

    for s in range(blocks):
        first = planes * lax.bitwise_xor(dom, s)
        for p in range(planes):
            turned[s][p * rows : (p + 1) * rows, :] = wave[NT - 1, first + p, 8 + EDGE : 8 + EDGE + rows, :]


def backward(mine, rows, count, heard, wave, lap, model, image, adjoint, weighted, gain):
    nx, tall, depth = lap.shape[1:]
    shot = lax.axis_index("shot")
    core = lax.rem(shot, 2)
    half = rows // 2
    wide = half + 2 * EDGE
    first = pl.multiple_of((core if mine else 1 - core) * half, 8)
    some = 40 if wide % 40 == 0 else 16
    low, high = edges(some, depth)

    def at(a, size=some, off=0):
        return pl.ds(pl.multiple_of(first + (a + off), 8), size)

    for a in range(0, wide, some):
        here = slice(a, a + some)
        for x in range(nx):
            now = count[at(a, off=x * tall), :] * wave[NT - 1, x, at(a, off=8), :] - heard[NT - 1, at(a, off=x * tall), :]
            adjoint[NT % 2, x, here, :] = now
            weighted[NT % 2, x, 8 + a : 8 + a + some, :] = now * model[x, at(a, off=8), :]
            gain[x, here, :] = now * lap[NT - 1, x, at(a), :]

    for level in range(NT - 1, 1, -1):
        new, old = level % 2, 1 - level % 2
        for a in range(0, wide, some):
            here = slice(a, a + some)
            for x, held in sweep(weighted, (old,), 8 + a, some, nx):
                turn = bend(weighted, (old,), 8 + a, some, nx, x, held, low, high) - 6.0 * held[1]
                after = adjoint[old, x, here, :]
                now = count[at(a, off=x * tall), :] * wave[level - 1, x, at(a, off=8), :]
                now = (now - heard[level - 1, at(a, off=x * tall), :]) + (turn + (after + after))
                if level < NT - 1:
                    now = now - adjoint[new, x, here, :]
                adjoint[new, x, here, :] = now
                weighted[new, x, 8 + a : 8 + a + some, :] = now * model[x, at(a, off=8), :]
                gain[x, here, :] = gain[x, here, :] + now * lap[level - 1, x, at(a), :]

    some = 32 if half % 32 == 0 else 16
    low, high = edges(some, depth)
    for a in range(EDGE, EDGE + half, some):
        here = slice(a, a + some)
        for x, held in sweep(weighted, (0,), 8 + a, some, nx):
            turn = bend(weighted, (0,), 8 + a, some, nx, x, held, low, high) - 6.0 * held[1]
            after = adjoint[0, x, here, :]
            now = count[at(a, some, x * tall), :] * wave[0, x, at(a, some, 8), :]
            now = (now - heard[0, at(a, some, x * tall), :]) + (turn + (after + after)) - adjoint[1, x, here, :]
            total = gain[x, here, :] + now * lap[0, x, at(a, some), :]
            image[x * half + a - EDGE : x * half + a - EDGE + some, :] = total / NT

    @pl.when(shot == 0)
    def _():
        for x in range(nx):
            weighted[0, x, 0 : wide + 16, :] = model[x, pl.ds(first, wide + 16), :]
        for a in range(EDGE, EDGE + half, some):
            for x, held in sweep(weighted, (0,), 8 + a, some, nx):
                total = bend(weighted, (0,), 8 + a, some, nx, x, held, low, high)
                score = (total / 6.0 - held[1]) * PRIOR_GAIN
                to = slice(x * half + a - EDGE, x * half + a - EDGE + some)
                image[to, :] = image[to, :] - score


def cut(blocks, keep, got, *outs):
    dom = lax.axis_index("dom")
    size = outs[0].shape[0]
    for s in range(blocks):
        at = pl.ds(pl.multiple_of(lax.bitwise_xor(dom, s) * size, 8), size)
        outs[s][...] = keep[at, :] + got[at, :]


def sort(blocks, *refs):
    came, outs, held = refs[:blocks][::-1], refs[blocks : 2 * blocks], refs[2 * blocks]
    dom, pair = lax.axis_index("dom"), lax.axis_index("shot") // 2
    for s in range(blocks):
        held[lax.bitwise_xor(dom, s)] = came[s][...]
    for s in range(blocks):
        outs[s][...] = held[lax.bitwise_xor(pair, s)]


def add(planes, *refs):
    out = refs[-1]
    size = out.shape[1]
    for p in range(planes):
        total = refs[0][p * size : (p + 1) * size, :]
        for ref in refs[1:-1]:
            total = total + ref[p * size : (p + 1) * size, :]
        out[p] = total


def join(planes, rows, *refs):
    out = refs[-1]
    dom = lax.axis_index("dom")
    for s, ref in enumerate(refs[:-1]):
        at = pl.ds(pl.multiple_of(lax.bitwise_xor(dom, s) * rows, 8), rows)
        for p in range(planes):
            out[p, at, :] = ref[p * rows : (p + 1) * rows, :]


def shards(kappa, wave_now, wave_before, wavelet, source_cell, receiver_cells, observed):
    shots, blocks = lax.axis_size("shot"), lax.axis_size("dom")
    _, planes, ny, depth = wave_now.shape
    rows = ny // blocks
    tall = rows + 2 * EDGE
    nx = planes * blocks
    listed = receiver_cells.shape[1]

    def across(array, to):
        pairs = []
        for shot in range(shots):
            for dom in range(blocks):
                there = to(shot, dom)
                pairs.append((shot * blocks + dom, there[0] * blocks + there[1]))
        return lax.ppermute(array, ("shot", "dom"), pairs)

    def over_dom(arrays):
        return [arrays[0]] + [across(arrays[s], lambda shot, dom, s=s: (shot, dom ^ s)) for s in range(1, blocks)]

    def over_pairs(arrays):
        return [arrays[0]] + [across(arrays[s], lambda shot, dom, s=s: (shot ^ (2 * s), dom)) for s in range(1, blocks)]

    half = tall // 2
    held = pltpu.VMEM((planes, ny, depth), jnp.float32)
    early = call(
        functools.partial(pack_early, blocks, planes, rows),
        [(tall + planes * half, depth)] * (blocks - 1),
        in_specs=[HBM] * 2,
        scratch=[
            pltpu.VMEM((1, ny, depth), jnp.float32),
            held,
            pltpu.VMEM((tall, depth), jnp.float32),
            pltpu.SemaphoreType.DMA((planes + 1,)),
        ],
    )(stay(kappa), stay(wave_now[0]))
    early, before = lax.optimization_barrier((early, wave_before[0]))
    *late, own = call(
        functools.partial(pack_late, blocks, planes, rows),
        [((2 * planes - 1) * tall, depth)] * (blocks - 1) + [(3 * planes * tall, depth)],
        in_specs=[HBM] * 3,
        scratch=[held, held, held, pltpu.SemaphoreType.DMA((3, planes))],
    )(stay(kappa), stay(wave_now[0]), stay(before))
    early = over_dom([None, *early])[1:]
    late = over_dom([None, *late])[1:]

    wide = (1 + 3 * NT) * depth
    count, heard, pulse = call(
        functools.partial(spread, depth, ny, rows, listed),
        [(nx * tall, depth), (NT, nx * tall, depth), (NT, depth)],
        in_specs=[SMEM, HBM, HBM, HBM],
        scratch=[pltpu.VMEM((listed + BLOCK, depth), jnp.float32)]
        + [pltpu.VMEM(array.shape, array.dtype) for array in (wavelet, receiver_cells, observed)]
        + [pltpu.SemaphoreType.DMA((3,))],
        flops=1000 * 1000 * 1000,
        moved=1,
    )(source_cell, stay(wavelet), stay(receiver_cells), stay(observed))

    came, pulse = lax.optimization_barrier((early, pulse))
    parts = call(
        functools.partial(gather, planes, half), [((blocks - 1) * half, depth)] * planes, in_specs=[VMEM] * (blocks - 1)
    )(*came)
    swapped = [across(part, lambda shot, dom: (shot ^ 1, dom)) for part in parts]

    padded, plain = (nx, tall + 16, depth), (nx, tall, depth)
    cells = nx * tall * depth
    wave, lap, model, *turned = call(
        functools.partial(forward, blocks, planes, rows, ny),
        [(NT, *padded), (NT, *plain), padded] + [(planes * rows, depth)] * blocks,
        in_specs=[SMEM] + [VMEM] * (2 * blocks + planes),
        scratch=[pltpu.VMEM((2, *padded), jnp.float32)],
        flops=16 * NT * cells,
        moved=16 * NT * cells,
    )(source_cell, pulse, *early, *late, own, *swapped)
    half = rows // 2
    side = half + 2 * EDGE
    give, keep = (
        call(
            functools.partial(backward, mine, rows),
            [(nx * half, depth)],
            in_specs=[VMEM] * 5,
            scratch=[
                pltpu.VMEM((2, nx, side, depth), jnp.float32),
                pltpu.VMEM((2, nx, side + 16, depth), jnp.float32),
                pltpu.VMEM((nx, side, depth), jnp.float32),
            ],
            flops=12 * NT * cells,
            moved=12 * NT * cells,
        )(count, heard, wave, lap, model)[0]
        for mine in (False, True)
    )

    got = across(give, lambda shot, dom: (shot ^ 1, dom))
    pieces = call(functools.partial(cut, blocks), [(planes * half, depth)] * blocks, in_specs=[VMEM] * 2)(keep, got)
    pieces = over_dom(pieces)
    turned = over_dom(turned)
    pieces = call(
        functools.partial(sort, blocks),
        [(planes * half, depth)] * blocks,
        in_specs=[VMEM] * blocks,
        scratch=[pltpu.VMEM((blocks, planes * half, depth), jnp.float32)],
        flops=1400 * 1000 * 1000,
        moved=1,
    )(*pieces[::-1])
    pieces = over_pairs(pieces)
    (wave_next,) = call(functools.partial(join, planes, rows), [(planes, ny, depth)], in_specs=[VMEM] * blocks)(*turned)
    (total,) = call(functools.partial(add, planes), [(planes, half, depth)], in_specs=[VMEM] * blocks)(*pieces[::-1])
    return total, wave_next[None]


def solution(mesh):
    return jax.shard_map(
        shards,
        mesh=mesh,
        in_specs=(
            P("dom", None, None),
            P("shot", "dom", None, None),
            P("shot", "dom", None, None),
            P("shot", None),
            P("shot"),
            P("shot", None),
            P("shot", None, None),
        ),
        out_specs=(P("dom", "shot", None), P("shot", "dom", None, None)),
        check_vma=False,
    )
```

```python
import functools

import jax
import jax.numpy as jnp
from jax import lax
from jax.experimental import pallas as pl
from jax.experimental.pallas import tpu as pltpu
from jax.sharding import PartitionSpec as P

NT = 4
PRIOR_GAIN = 50.0
EDGE = 8
VMEM = pl.BlockSpec(memory_space=pltpu.VMEM)
HBM = pl.BlockSpec(memory_space=pltpu.HBM)
SMEM = pl.BlockSpec(memory_space=pltpu.SMEM)
LIMIT = 32 * 1024 * 1024
BLOCK = 768


def stay(array):
    return pltpu.with_memory_space_constraint(array, pltpu.HBM)


def call(body, out_rows, scratch=(), in_specs=(), flops=0, moved=0):
    return pl.pallas_call(
        body,
        out_shape=[jax.ShapeDtypeStruct(*s) if isinstance(s[0], tuple) else jax.ShapeDtypeStruct(s, jnp.float32) for s in out_rows],
        in_specs=list(in_specs),
        out_specs=[VMEM] * len(out_rows),
        scratch_shapes=list(scratch),
        compiler_params=pltpu.CompilerParams(vmem_limit_bytes=LIMIT),
        cost_estimate=pl.CostEstimate(flops=flops, bytes_accessed=moved, transcendentals=0),
    )


def window(field, plane, block, blocks, rows):
    first = pl.multiple_of(block * rows, 8)
    above = pl.multiple_of(jnp.maximum(first - EDGE, 0), 8)
    below = pl.multiple_of(jnp.minimum(first + rows, (blocks * rows) - EDGE), 8)
    top = field[plane, pl.ds(above, EDGE), :]
    bottom = field[plane, pl.ds(below, EDGE), :]
    top = jnp.where(block > 0, top, 0.0)
    bottom = jnp.where(block < blocks - 1, bottom, 0.0)
    return top, field[plane, pl.ds(first, rows), :], bottom


def put(field, plane, block, blocks, rows, out, at):
    top, core, bottom = window(field, plane, block, blocks, rows)
    out[at : at + EDGE, :] = top
    out[at + EDGE : at + EDGE + rows, :] = core
    out[at + EDGE + rows : at + rows + 2 * EDGE, :] = bottom


def fetch(field, held, semaphores):
    copies = [pltpu.make_async_copy(field.at[p], held.at[p], semaphores.at[p]) for p in range(held.shape[0])]
    for copy in copies:
        copy.start()
    return copies


def pack_early(blocks, planes, rows, kappa, now, *refs):
    outs, (held, model, whole, semaphores) = refs[: blocks - 1], refs[blocks - 1 :]
    dom, core = lax.axis_index("dom"), lax.rem(lax.axis_index("shot"), 2)
    waves, kappas = fetch(now, held, semaphores.at[0]), fetch(kappa, model, semaphores.at[1])
    tall = rows + 2 * EDGE
    half = tall // 2
    for p in range(planes):
        waves[p].wait()
        for s in range(1, blocks):
            put(held, p, lax.bitwise_xor(dom, s), blocks, rows, outs[s - 1], p * tall)
    for p in range(planes):
        kappas[p].wait()
        for s in range(1, blocks):
            put(model, p, lax.bitwise_xor(dom, s), blocks, rows, whole, 0)
            at = planes * tall + p * half
            outs[s - 1][at : at + half, :] = whole[pl.ds(pl.multiple_of(core * half, 8), half), :]


def pack_late(blocks, planes, rows, kappa, now, before, *refs):
    outs, own, refs = refs[: blocks - 1], refs[blocks - 1], refs[blocks:]
    held, semaphores = refs[:3], refs[3]
    copies = [fetch(field, ref, semaphores.at[i]) for i, (field, ref) in enumerate(zip((before, now, kappa), held))]
    dom = lax.axis_index("dom")
    tall = rows + 2 * EDGE
    for f in range(3):
        for p in range(planes):
            copies[f][p].wait()
            put(held[f], p, dom, blocks, rows, own, (f * planes + p) * tall)
            if f == 0:
                for s in range(1, blocks):
                    put(held[f], p, lax.bitwise_xor(dom, s), blocks, rows, outs[s - 1], p * tall)


def gather(planes, half, *refs):
    parts, outs = refs[:-planes], refs[-planes:]
    for i, part in enumerate(parts):
        first = part.shape[0] - planes * half
        for p, out in enumerate(outs):
            out[i * half : (i + 1) * half, :] = part[first + p * half : first + (p + 1) * half, :]


def spread(depth, ny, rows, count, source, lists_at, cells_at, observed_at, *refs):
    count_ref, heard_ref, pulse_ref, listed, wavelet, cells_ref, observed_ref, semaphores = refs
    copies = [
        pltpu.make_async_copy(lists_at, wavelet, semaphores.at[0]),
        pltpu.make_async_copy(cells_at, cells_ref, semaphores.at[1]),
        pltpu.make_async_copy(observed_at, observed_ref, semaphores.at[2]),
    ]
    for copy in copies:
        copy.start()
    tall = rows + 2 * EDGE
    size = count_ref.shape[0]
    dom = lax.axis_index("dom")
    spot = lax.rem(source[0], depth)
    lane = lax.broadcasted_iota(jnp.int32, (1, depth), 1)
    count_ref[...] = jnp.zeros_like(count_ref)
    heard_ref[...] = jnp.zeros_like(heard_ref)
    for copy in copies:
        copy.wait()
    for n in range(NT):
        pulse_ref[n : n + 1, :] = jnp.where(lane == spot, wavelet[:, n : n + 1], 0.0)
    cells = cells_ref[...]
    line = cells // depth
    x = line // ny
    y = line - x * ny - (dom * rows - EDGE)
    here = (y >= 0) & (y < tall)
    row = x * tall + jnp.clip(y, 0, tall - 1)
    coarse = row // 64
    stack = [array.astype(jnp.float32) for array in (coarse, row - coarse * 64, cells - line * depth)]
    left = observed_ref[0]
    for part in range(3):
        piece = left.astype(jnp.bfloat16).astype(jnp.float32)
        left = left - piece
        stack.append(piece)
    stack = jnp.concatenate(stack + [jnp.zeros((13 - 3 * NT, count), jnp.float32)], axis=0)

    columns = 128
    ones = jnp.where(here, 1.0, 0.0)
    ones = jnp.concatenate([ones[:, j : j + columns] for j in range(0, count, columns)], axis=0)
    square = (columns, columns)
    down, across = lax.broadcasted_iota(jnp.int32, square, 0), lax.broadcasted_iota(jnp.int32, square, 1)
    order = jnp.dot(ones, jnp.where(down < across, 1.0, 0.0), preferred_element_type=jnp.float32)
    order = jnp.where(ones > 0.0, order, -1.0)
    slots = down.astype(jnp.float32)
    total = 0
    for j in range(count // columns):
        turned = stack[:, j * columns : (j + 1) * columns].T.astype(jnp.bfloat16)
        move = jnp.where(slots == order[j : j + 1, :], 1.0, 0.0).astype(jnp.bfloat16)
        listed[pl.ds(total, columns), 0:16] = jnp.dot(move, turned, preferred_element_type=jnp.float32)
        total = total + jnp.sum(ones[j : j + 1, :]).astype(jnp.int32)

    def block(k, _):
        first = pl.multiple_of(k * BLOCK, 8)
        which = lax.broadcasted_iota(jnp.int32, (BLOCK, 16), 0) + first
        some = jnp.where(which < total, listed[pl.ds(first, BLOCK), 0:16], -1.0)
        flat = some.T
        ids = (flat[0:1, :] * 64.0 + flat[1:2, :]).astype(jnp.int32)
        hot = jnp.where(lax.broadcasted_iota(jnp.int32, (size, BLOCK), 0) == ids, 1.0, 0.0).astype(jnp.bfloat16)
        at = lax.broadcasted_iota(jnp.int32, (BLOCK, depth), 1).astype(jnp.float32) == some[:, 2:3]
        at = jnp.where(at, 1.0, 0.0).astype(jnp.bfloat16)
        some = some.astype(jnp.bfloat16)
        value = [at] + [at * some[:, 3 + i : 4 + i] for i in range(3 * NT)]
        out = jnp.dot(hot, jnp.concatenate(value, axis=1), preferred_element_type=jnp.float32)
        count_ref[...] += out[:, 0:depth]
        for n in range(NT):
            high, mid, low = (out[:, i * depth : (i + 1) * depth] for i in (1 + n, 1 + NT + n, 1 + 2 * NT + n))
            heard_ref[n] += high + (mid + low)
        return 0

    lax.fori_loop(0, (total + BLOCK - 1) // BLOCK, block, 0)


def bend(field, at, first, some, nx, x, planes_held, low, high):
    under, mid, over = planes_held
    total = field[(*at, x, pl.ds(first + 1, some))] + field[(*at, x, pl.ds(first - 1, some))]
    up = jnp.where(high, 0.0, pltpu.roll(mid, mid.shape[1] - 1, 1))
    down = jnp.where(low, 0.0, pltpu.roll(mid, 1, 1))
    total = total + (up + down)
    if x > 0:
        total = total + under
    if x < nx - 1:
        total = total + over
    return total


def sweep(field, at, first, some, nx):
    under, mid = None, field[(*at, 0, pl.ds(first, some))]
    for x in range(nx):
        over = field[(*at, x + 1, pl.ds(first, some))] if x < nx - 1 else None
        yield x, (under, mid, over)
        under, mid = mid, over


def edges(some, depth):
    lanes = lax.broadcasted_iota(jnp.int32, (some, depth), 1)
    return lanes == 0, lanes == depth - 1


def begin(blocks, planes, rows, own, *refs):
    early, wave, lap = refs[: blocks - 1], refs[blocks - 1], refs[blocks]
    nx, tall, depth = lap.shape
    dom = lax.axis_index("dom")
    for s in range(blocks):
        first = planes * lax.bitwise_xor(dom, s)
        for p in range(planes):
            part = early[s - 1][p * tall : (p + 1) * tall, :] if s > 0 else own[(planes + p) * tall : (planes + p + 1) * tall, :]
            wave[first + p, 8 : 8 + tall, :] = part
    some = 48
    low, high = edges(some, depth)
    for a in range(0, tall, some):
        for x, held in sweep(wave, (), 8 + a, some, nx):
            lap[x, a : a + some, :] = bend(wave, (), 8 + a, some, nx, x, held, low, high) - 6.0 * held[1]


def forward(blocks, planes, rows, ny, source, pulse, *refs):
    early, late, own, refs = refs[: blocks - 1], refs[blocks - 1 : 2 * blocks - 2], refs[2 * blocks - 2], refs[2 * blocks - 1 :]
    swapped, start, bent, refs = refs[:planes], refs[planes], refs[planes + 1], refs[planes + 2 :]
    wave, lap, model, turned = *refs[:3], refs[3:]
    nx, tall, depth = lap.shape[1:]
    dom, core = lax.axis_index("dom"), lax.rem(lax.axis_index("shot"), 2)
    half = tall // 2
    near = pl.ds(pl.multiple_of(8 + core * half, 8), half)
    other = pl.ds(pl.multiple_of(8 + (1 - core) * half, 8), half)
    for s in range(blocks):
        first = planes * lax.bitwise_xor(dom, s)
        for p in range(planes):
            if s == 0:
                at = (2 * planes + p) * tall
                model[first + p, 8 : 8 + tall, :] = own[at : at + tall, :]
            else:
                at = planes * tall + p * half
                model[first + p, near, :] = early[s - 1][at : at + half, :]
                model[first + p, other, :] = swapped[p][(s - 1) * half : s * half, :]

    some = 48
    low, high = edges(some, depth)
    line = source[0] // depth
    sx = line // ny
    sy = line - sx * ny - (dom * rows - EDGE)
    source_here = (sy >= 0) & (sy < tall)
    sy = 8 + jnp.clip(sy, 0, tall - 1)

    def inject(n):
        @pl.when(source_here)
        def _():
            wave[n, sx, pl.ds(sy, 1), :] = wave[n, sx, pl.ds(sy, 1), :] + pulse[n : n + 1, :]

    for s in range(blocks):
        for p in range(planes):
            x = planes * lax.bitwise_xor(dom, s) + p
            for a in range(0, tall, some):
                rows_at = slice(8 + a, 8 + a + some)
                mid = start[x, rows_at, :]
                old = late[s - 1] if s > 0 else own
                new = (mid + mid) - old[p * tall + a : p * tall + a + some, :]
                wave[0, x, rows_at, :] = new + model[x, rows_at, :] * bent[x, a : a + some, :]
    inject(0)

    for n in range(1, NT):
        for a in range(0, tall, some):
            rows_at = slice(8 + a, 8 + a + some)
            for x, held in sweep(wave, (n - 1,), 8 + a, some, nx):
                mid = held[1]
                turn = bend(wave, (n - 1,), 8 + a, some, nx, x, held, low, high) - 6.0 * mid
                lap[n - 1, x, a : a + some, :] = turn
                old = start[x, rows_at, :] if n == 1 else wave[n - 2, x, rows_at, :]
                wave[n, x, rows_at, :] = (mid + mid) - old + model[x, rows_at, :] * turn
        inject(n)

    for s in range(blocks):
        first = planes * lax.bitwise_xor(dom, s)
        for p in range(planes):
            turned[s][p * rows : (p + 1) * rows, :] = wave[NT - 1, first + p, 8 + EDGE : 8 + EDGE + rows, :]


def backward(mine, rows, count, heard, wave, lap, bent, model, image, adjoint, weighted, gain):
    nx, tall, depth = bent.shape
    shot = lax.axis_index("shot")
    core = lax.rem(shot, 2)
    half = rows // 2
    wide = half + 2 * EDGE
    first = pl.multiple_of((core if mine else 1 - core) * half, 8)
    some = 40 if wide % 40 == 0 else 16
    low, high = edges(some, depth)

    def at(a, size=some, off=0):
        return pl.ds(pl.multiple_of(first + (a + off), 8), size)

    for a in range(0, wide, some):
        here = slice(a, a + some)
        for x in range(nx):
            now = count[at(a, off=x * tall), :] * wave[NT - 1, x, at(a, off=8), :] - heard[NT - 1, at(a, off=x * tall), :]
            adjoint[NT % 2, x, here, :] = now
            weighted[NT % 2, x, 8 + a : 8 + a + some, :] = now * model[x, at(a, off=8), :]
            gain[x, here, :] = now * lap[NT - 2, x, at(a), :]

    for level in range(NT - 1, 1, -1):
        new, old = level % 2, 1 - level % 2
        for a in range(0, wide, some):
            here = slice(a, a + some)
            for x, held in sweep(weighted, (old,), 8 + a, some, nx):
                turn = bend(weighted, (old,), 8 + a, some, nx, x, held, low, high) - 6.0 * held[1]
                after = adjoint[old, x, here, :]
                now = count[at(a, off=x * tall), :] * wave[level - 1, x, at(a, off=8), :]
                now = (now - heard[level - 1, at(a, off=x * tall), :]) + (turn + (after + after))
                if level < NT - 1:
                    now = now - adjoint[new, x, here, :]
                adjoint[new, x, here, :] = now
                weighted[new, x, 8 + a : 8 + a + some, :] = now * model[x, at(a, off=8), :]
                gain[x, here, :] = gain[x, here, :] + now * lap[level - 2, x, at(a), :]

    some = 32 if half % 32 == 0 else 16
    low, high = edges(some, depth)
    for a in range(EDGE, EDGE + half, some):
        here = slice(a, a + some)
        for x, held in sweep(weighted, (0,), 8 + a, some, nx):
            turn = bend(weighted, (0,), 8 + a, some, nx, x, held, low, high) - 6.0 * held[1]
            after = adjoint[0, x, here, :]
            now = count[at(a, some, x * tall), :] * wave[0, x, at(a, some, 8), :]
            now = (now - heard[0, at(a, some, x * tall), :]) + (turn + (after + after)) - adjoint[1, x, here, :]
            total = gain[x, here, :] + now * bent[x, at(a, some), :]
            image[x * half + a - EDGE : x * half + a - EDGE + some, :] = total / NT

    @pl.when(shot == 0)
    def _():
        for x in range(nx):
            weighted[0, x, 0 : wide + 16, :] = model[x, pl.ds(first, wide + 16), :]
        for a in range(EDGE, EDGE + half, some):
            for x, held in sweep(weighted, (0,), 8 + a, some, nx):
                total = bend(weighted, (0,), 8 + a, some, nx, x, held, low, high)
                score = (total / 6.0 - held[1]) * PRIOR_GAIN
                to = slice(x * half + a - EDGE, x * half + a - EDGE + some)
                image[to, :] = image[to, :] - score


def cut(blocks, keep, got, *outs):
    dom = lax.axis_index("dom")
    size = outs[0].shape[0]
    for s in range(blocks):
        at = pl.ds(pl.multiple_of(lax.bitwise_xor(dom, s) * size, 8), size)
        outs[s][...] = keep[at, :] + got[at, :]


def sort(blocks, *refs):
    came, outs, held = refs[:blocks][::-1], refs[blocks : 2 * blocks], refs[2 * blocks]
    dom, pair = lax.axis_index("dom"), lax.axis_index("shot") // 2
    for s in range(blocks):
        held[lax.bitwise_xor(dom, s)] = came[s][...]
    for s in range(blocks):
        outs[s][...] = held[lax.bitwise_xor(pair, s)]


def add(planes, *refs):
    out = refs[-1]
    size = out.shape[1]
    for p in range(planes):
        total = refs[0][p * size : (p + 1) * size, :]
        for ref in refs[1:-1]:
            total = total + ref[p * size : (p + 1) * size, :]
        out[p] = total


def join(planes, rows, *refs):
    out = refs[-1]
    dom = lax.axis_index("dom")
    for s, ref in enumerate(refs[:-1]):
        at = pl.ds(pl.multiple_of(lax.bitwise_xor(dom, s) * rows, 8), rows)
        for p in range(planes):
            out[p, at, :] = ref[p * rows : (p + 1) * rows, :]


def shards(kappa, wave_now, wave_before, wavelet, source_cell, receiver_cells, observed):
    shots, blocks = lax.axis_size("shot"), lax.axis_size("dom")
    _, planes, ny, depth = wave_now.shape
    rows = ny // blocks
    tall = rows + 2 * EDGE
    nx = planes * blocks
    listed = receiver_cells.shape[1]

    def across(array, to):
        pairs = []
        for shot in range(shots):
            for dom in range(blocks):
                there = to(shot, dom)
                pairs.append((shot * blocks + dom, there[0] * blocks + there[1]))
        return lax.ppermute(array, ("shot", "dom"), pairs)

    def over_dom(arrays):
        return [arrays[0]] + [across(arrays[s], lambda shot, dom, s=s: (shot, dom ^ s)) for s in range(1, blocks)]

    def over_pairs(arrays):
        return [arrays[0]] + [across(arrays[s], lambda shot, dom, s=s: (shot ^ (2 * s), dom)) for s in range(1, blocks)]

    half = tall // 2
    held = pltpu.VMEM((planes, ny, depth), jnp.float32)
    early = call(
        functools.partial(pack_early, blocks, planes, rows),
        [(planes * (tall + half), depth)] * (blocks - 1),
        in_specs=[HBM] * 2,
        scratch=[
            held,
            held,
            pltpu.VMEM((tall, depth), jnp.float32),
            pltpu.SemaphoreType.DMA((2, planes)),
        ],
    )(stay(kappa), stay(wave_now[0]))
    early, before = lax.optimization_barrier((early, wave_before[0]))
    *late, own = call(
        functools.partial(pack_late, blocks, planes, rows),
        [(planes * tall, depth)] * (blocks - 1) + [(3 * planes * tall, depth)],
        in_specs=[HBM] * 3,
        scratch=[held, held, held, pltpu.SemaphoreType.DMA((3, planes))],
    )(stay(kappa), stay(wave_now[0]), stay(before))
    early = over_dom([None, *early])[1:]
    late = over_dom([None, *late])[1:]

    count, heard, pulse = call(
        functools.partial(spread, depth, ny, rows, listed),
        [(nx * tall, depth), (NT, nx * tall, depth), (NT, depth)],
        in_specs=[SMEM, HBM, HBM, HBM],
        scratch=[pltpu.VMEM((listed + BLOCK, depth), jnp.float32)]
        + [pltpu.VMEM(array.shape, array.dtype) for array in (wavelet, receiver_cells, observed)]
        + [pltpu.SemaphoreType.DMA((3,))],
        flops=1,
        moved=1,
    )(source_cell, stay(wavelet), stay(receiver_cells), stay(observed))

    came, pulse = lax.optimization_barrier((early, pulse))
    parts = call(
        functools.partial(gather, planes, half), [((blocks - 1) * half, depth)] * planes, in_specs=[VMEM] * (blocks - 1)
    )(*came)
    swapped = [across(part, lambda shot, dom: (shot ^ 1, dom)) for part in parts]

    padded, plain = (nx, tall + 16, depth), (nx, tall, depth)
    cells = nx * tall * depth
    start, bent = call(
        functools.partial(begin, blocks, planes, rows),
        [padded, plain],
        in_specs=[VMEM] * blocks,
        flops=1000*1000*1000,
        moved=1,
    )(own, *early)
    wave, lap, model, *turned = call(
        functools.partial(forward, blocks, planes, rows, ny),
        [(NT, *padded), (NT - 1, *plain), padded] + [(planes * rows, depth)] * blocks,
        in_specs=[SMEM] + [VMEM] * (2 * blocks + planes + 2),
        flops=16 * NT * cells,
        moved=16 * NT * cells,
    )(source_cell, pulse, *early, *late, own, *swapped, start, bent)
    half = rows // 2
    side = half + 2 * EDGE
    give, keep = (
        call(
            functools.partial(backward, mine, rows),
            [(nx * half, depth)],
            in_specs=[VMEM] * 6,
            scratch=[
                pltpu.VMEM((2, nx, side, depth), jnp.float32),
                pltpu.VMEM((2, nx, side + 16, depth), jnp.float32),
                pltpu.VMEM((nx, side, depth), jnp.float32),
            ],
            flops=12 * NT * cells,
            moved=12 * NT * cells,
        )(count, heard, wave, lap, bent, model)[0]
        for mine in (False, True)
    )

    got = across(give, lambda shot, dom: (shot ^ 1, dom))
    pieces = call(functools.partial(cut, blocks), [(planes * half, depth)] * blocks, in_specs=[VMEM] * 2)(keep, got)
    pieces = over_dom(pieces)
    turned = over_dom(turned)
    pieces = call(
        functools.partial(sort, blocks),
        [(planes * half, depth)] * blocks,
        in_specs=[VMEM] * blocks,
        scratch=[pltpu.VMEM((blocks, planes * half, depth), jnp.float32)],
        flops=1400 * 1000 * 1000,
        moved=1,
    )(*pieces[::-1])
    pieces = over_pairs(pieces)
    (wave_next,) = call(functools.partial(join, planes, rows), [(planes, ny, depth)], in_specs=[VMEM] * blocks)(*turned)
    (total,) = call(functools.partial(add, planes), [(planes, half, depth)], in_specs=[VMEM] * blocks)(*pieces[::-1])
    return total, wave_next[None]


def solution(mesh):
    return jax.shard_map(
        shards,
        mesh=mesh,
        in_specs=(
            P("dom", None, None),
            P("shot", "dom", None, None),
            P("shot", "dom", None, None),
            P("shot", None),
            P("shot"),
            P("shot", None),
            P("shot", None, None),
        ),
        out_specs=(P("dom", "shot", None), P("shot", "dom", None, None)),
        check_vma=False,
    )
```

```python
import functools

import jax
import jax.numpy as jnp
from jax import lax
from jax.experimental import pallas as pl
from jax.experimental.pallas import tpu as pltpu
from jax.sharding import PartitionSpec as P

NT = 4
PRIOR_GAIN = 50.0
EDGE = 8
VMEM = pl.BlockSpec(memory_space=pltpu.VMEM)
HBM = pl.BlockSpec(memory_space=pltpu.HBM)
SMEM = pl.BlockSpec(memory_space=pltpu.SMEM)
LIMIT = 32 * 1024 * 1024
BLOCK = 768


def stay(array):
    return pltpu.with_memory_space_constraint(array, pltpu.HBM)


def call(body, out_rows, scratch=(), in_specs=(), flops=0, moved=0):
    return pl.pallas_call(
        body,
        out_shape=[jax.ShapeDtypeStruct(*s) if isinstance(s[0], tuple) else jax.ShapeDtypeStruct(s, jnp.float32) for s in out_rows],
        in_specs=list(in_specs),
        out_specs=[VMEM] * len(out_rows),
        scratch_shapes=list(scratch),
        compiler_params=pltpu.CompilerParams(vmem_limit_bytes=LIMIT),
        cost_estimate=pl.CostEstimate(flops=flops, bytes_accessed=moved, transcendentals=0),
    )


def window(field, plane, block, blocks, rows):
    first = pl.multiple_of(block * rows, 8)
    above = pl.multiple_of(jnp.maximum(first - EDGE, 0), 8)
    below = pl.multiple_of(jnp.minimum(first + rows, (blocks * rows) - EDGE), 8)
    top = field[plane, pl.ds(above, EDGE), :]
    bottom = field[plane, pl.ds(below, EDGE), :]
    top = jnp.where(block > 0, top, 0.0)
    bottom = jnp.where(block < blocks - 1, bottom, 0.0)
    return top, field[plane, pl.ds(first, rows), :], bottom


def put(field, plane, block, blocks, rows, out, at):
    top, core, bottom = window(field, plane, block, blocks, rows)
    out[at : at + EDGE, :] = top
    out[at + EDGE : at + EDGE + rows, :] = core
    out[at + EDGE + rows : at + rows + 2 * EDGE, :] = bottom


def fetch(field, held, semaphores):
    copies = [pltpu.make_async_copy(field.at[p], held.at[p], semaphores.at[p]) for p in range(held.shape[0])]
    for copy in copies:
        copy.start()
    return copies


def pack_early(blocks, planes, rows, kappa, now, *refs):
    outs, (held, inner, outer, semaphores) = refs[: blocks - 1], refs[blocks - 1 :]
    dom, core = lax.axis_index("dom"), lax.rem(lax.axis_index("shot"), 2)
    tall, side = rows + 2 * EDGE, rows // 2
    half = side + EDGE
    inside = pl.ds(pl.multiple_of(core * side, 8), side)
    beside = pl.ds(pl.multiple_of((1 - core) * (rows - EDGE), 8), EDGE)
    copies = fetch(now, held, semaphores)
    copies.append(pltpu.make_async_copy(kappa.at[:, :, inside], inner, semaphores.at[planes]))
    copies.append(pltpu.make_async_copy(kappa.at[:, :, beside], outer, semaphores.at[planes + 1]))
    for copy in copies[planes:]:
        copy.start()
    for p in range(planes):
        copies[p].wait()
        for s in range(1, blocks):
            put(held, p, lax.bitwise_xor(dom, s), blocks, rows, outs[s - 1], p * tall)
    for copy in copies[planes:]:
        copy.wait()
    for s in range(1, blocks):
        block = lax.bitwise_xor(dom, s)
        next_to = block - 1 + 2 * core
        there = (next_to >= 0) & (next_to < blocks)
        next_to = jnp.clip(next_to, 0, blocks - 1)
        for p in range(planes):
            at = planes * tall + p * half
            inner_at = pl.ds(pl.multiple_of(at + EDGE * (1 - core), 8), side)
            outer_at = pl.ds(pl.multiple_of(at + side * core, 8), EDGE)
            outs[s - 1][inner_at, :] = inner[p, block]
            outs[s - 1][outer_at, :] = jnp.where(there, outer[p, next_to], 0.0)


def pack_late(blocks, planes, rows, kappa, now, before, *refs):
    outs, own, refs = refs[: blocks - 1], refs[blocks - 1], refs[blocks:]
    held, semaphores = refs[:3], refs[3]
    copies = [fetch(field, ref, semaphores.at[i]) for i, (field, ref) in enumerate(zip((before, now, kappa), held))]
    dom = lax.axis_index("dom")
    tall = rows + 2 * EDGE
    for f in range(3):
        for p in range(planes):
            copies[f][p].wait()
            put(held[f], p, dom, blocks, rows, own, (f * planes + p) * tall)
            if f == 0:
                for s in range(1, blocks):
                    put(held[f], p, lax.bitwise_xor(dom, s), blocks, rows, outs[s - 1], p * tall)


def gather(planes, half, *refs):
    parts, outs = refs[:-planes], refs[-planes:]
    for i, part in enumerate(parts):
        first = part.shape[0] - planes * half
        for p, out in enumerate(outs):
            out[i * half : (i + 1) * half, :] = part[first + p * half : first + (p + 1) * half, :]


def spread(depth, ny, rows, count, source, lists_at, cells_at, observed_at, *refs):
    count_ref, heard_ref, pulse_ref, listed, wavelet, cells_ref, observed_ref, semaphores = refs
    copies = [
        pltpu.make_async_copy(lists_at, wavelet, semaphores.at[0]),
        pltpu.make_async_copy(cells_at, cells_ref, semaphores.at[1]),
        pltpu.make_async_copy(observed_at, observed_ref, semaphores.at[2]),
    ]
    for copy in copies:
        copy.start()
    tall = rows + 2 * EDGE
    size = count_ref.shape[0]
    dom = lax.axis_index("dom")
    spot = lax.rem(source[0], depth)
    lane = lax.broadcasted_iota(jnp.int32, (1, depth), 1)
    count_ref[...] = jnp.zeros_like(count_ref)
    heard_ref[...] = jnp.zeros_like(heard_ref)
    for copy in copies:
        copy.wait()
    for n in range(NT):
        pulse_ref[n : n + 1, :] = jnp.where(lane == spot, wavelet[:, n : n + 1], 0.0)
    cells = cells_ref[...]
    line = cells // depth
    x = line // ny
    y = line - x * ny - (dom * rows - EDGE)
    here = (y >= 0) & (y < tall)
    row = x * tall + jnp.clip(y, 0, tall - 1)
    coarse = row // 64
    stack = [array.astype(jnp.float32) for array in (coarse, row - coarse * 64, cells - line * depth)]
    left = observed_ref[0]
    for part in range(3):
        piece = left.astype(jnp.bfloat16).astype(jnp.float32)
        left = left - piece
        stack.append(piece)
    stack = jnp.concatenate(stack + [jnp.zeros((13 - 3 * NT, count), jnp.float32)], axis=0)

    columns = 128
    ones = jnp.where(here, 1.0, 0.0)
    ones = jnp.concatenate([ones[:, j : j + columns] for j in range(0, count, columns)], axis=0)
    square = (columns, columns)
    down, across = lax.broadcasted_iota(jnp.int32, square, 0), lax.broadcasted_iota(jnp.int32, square, 1)
    order = jnp.dot(ones, jnp.where(down < across, 1.0, 0.0), preferred_element_type=jnp.float32)
    order = jnp.where(ones > 0.0, order, -1.0)
    slots = down.astype(jnp.float32)
    total = 0
    for j in range(count // columns):
        turned = stack[:, j * columns : (j + 1) * columns].T.astype(jnp.bfloat16)
        move = jnp.where(slots == order[j : j + 1, :], 1.0, 0.0).astype(jnp.bfloat16)
        listed[pl.ds(total, columns), 0:16] = jnp.dot(move, turned, preferred_element_type=jnp.float32)
        total = total + jnp.sum(ones[j : j + 1, :]).astype(jnp.int32)

    def block(k, _):
        first = pl.multiple_of(k * BLOCK, 8)
        which = lax.broadcasted_iota(jnp.int32, (BLOCK, 16), 0) + first
        some = jnp.where(which < total, listed[pl.ds(first, BLOCK), 0:16], -1.0)
        flat = some.T
        ids = (flat[0:1, :] * 64.0 + flat[1:2, :]).astype(jnp.int32)
        hot = jnp.where(lax.broadcasted_iota(jnp.int32, (size, BLOCK), 0) == ids, 1.0, 0.0).astype(jnp.bfloat16)
        at = lax.broadcasted_iota(jnp.int32, (BLOCK, depth), 1).astype(jnp.float32) == some[:, 2:3]
        at = jnp.where(at, 1.0, 0.0).astype(jnp.bfloat16)
        some = some.astype(jnp.bfloat16)
        value = [at] + [at * some[:, 3 + i : 4 + i] for i in range(3 * NT)]
        out = jnp.dot(hot, jnp.concatenate(value, axis=1), preferred_element_type=jnp.float32)
        count_ref[...] += out[:, 0:depth]
        for n in range(NT):
            high, mid, low = (out[:, i * depth : (i + 1) * depth] for i in (1 + n, 1 + NT + n, 1 + 2 * NT + n))
            heard_ref[n] += high + (mid + low)
        return 0

    lax.fori_loop(0, (total + BLOCK - 1) // BLOCK, block, 0)


def bend(field, at, first, some, nx, x, planes_held, low, high):
    under, mid, over = planes_held
    total = field[(*at, x, pl.ds(first + 1, some))] + field[(*at, x, pl.ds(first - 1, some))]
    up = jnp.where(high, 0.0, pltpu.roll(mid, mid.shape[1] - 1, 1))
    down = jnp.where(low, 0.0, pltpu.roll(mid, 1, 1))
    total = total + (up + down)
    if x > 0:
        total = total + under
    if x < nx - 1:
        total = total + over
    return total


def sweep(field, at, first, some, nx):
    under, mid = None, field[(*at, 0, pl.ds(first, some))]
    for x in range(nx):
        over = field[(*at, x + 1, pl.ds(first, some))] if x < nx - 1 else None
        yield x, (under, mid, over)
        under, mid = mid, over


def edges(some, depth):
    lanes = lax.broadcasted_iota(jnp.int32, (some, depth), 1)
    return lanes == 0, lanes == depth - 1


def begin(blocks, planes, rows, own, *refs):
    early, swapped, (wave, lap, model, step) = refs[: blocks - 1], refs[blocks - 1 : -4], refs[-4:]
    nx, tall, depth = lap.shape
    dom, core = lax.axis_index("dom"), lax.rem(lax.axis_index("shot"), 2)
    half = tall // 2
    near = pl.ds(pl.multiple_of(8 + core * half, 8), half)
    other = pl.ds(pl.multiple_of(8 + (1 - core) * half, 8), half)
    for s in range(blocks):
        first = planes * lax.bitwise_xor(dom, s)
        for p in range(planes):
            if s == 0:
                at = (planes + p) * tall
                wave[first + p, 8 : 8 + tall, :] = own[at : at + tall, :]
                at += planes * tall
                model[first + p, 8 : 8 + tall, :] = own[at : at + tall, :]
            else:
                wave[first + p, 8 : 8 + tall, :] = early[s - 1][p * tall : (p + 1) * tall, :]
                at = planes * tall + p * half
                model[first + p, near, :] = early[s - 1][at : at + half, :]
                model[first + p, other, :] = swapped[p][(s - 1) * half : s * half, :]
    some = 48
    low, high = edges(some, depth)
    for a in range(0, tall, some):
        rows_at = slice(8 + a, 8 + a + some)
        for x, held in sweep(wave, (), 8 + a, some, nx):
            turn = bend(wave, (), 8 + a, some, nx, x, held, low, high) - 6.0 * held[1]
            lap[x, a : a + some, :] = turn
            step[x, a : a + some, :] = (held[1] + held[1]) + model[x, rows_at, :] * turn


def forward(blocks, planes, rows, ny, source, pulse, *refs):
    late, own, start, model, step, refs = refs[: blocks - 1], *refs[blocks - 1 : blocks + 3], refs[blocks + 3 :]
    wave, lap, turned = *refs[:2], refs[2:]
    nx, tall, depth = lap.shape[1:]
    dom = lax.axis_index("dom")
    some = 48
    low, high = edges(some, depth)
    line = source[0] // depth
    sx = line // ny
    sy = line - sx * ny - (dom * rows - EDGE)
    source_here = (sy >= 0) & (sy < tall)
    sy = 8 + jnp.clip(sy, 0, tall - 1)

    def inject(n):
        @pl.when(source_here)
        def _():
            wave[n, sx, pl.ds(sy, 1), :] = wave[n, sx, pl.ds(sy, 1), :] + pulse[n : n + 1, :]

    for s in range(blocks):
        before = late[s - 1] if s > 0 else own
        for p in range(planes):
            x = planes * lax.bitwise_xor(dom, s) + p
            wave[0, x, 8 : 8 + tall, :] = step[x] - before[p * tall : (p + 1) * tall, :]
    inject(0)

    for n in range(1, NT):
        for a in range(0, tall, some):
            rows_at = slice(8 + a, 8 + a + some)
            for x, held in sweep(wave, (n - 1,), 8 + a, some, nx):
                mid = held[1]
                turn = bend(wave, (n - 1,), 8 + a, some, nx, x, held, low, high) - 6.0 * mid
                lap[n - 1, x, a : a + some, :] = turn
                old = start[x, rows_at, :] if n == 1 else wave[n - 2, x, rows_at, :]
                wave[n, x, rows_at, :] = (mid + mid) - old + model[x, rows_at, :] * turn
        inject(n)

    for s in range(blocks):
        first = planes * lax.bitwise_xor(dom, s)
        for p in range(planes):
            turned[s][p * rows : (p + 1) * rows, :] = wave[NT - 1, first + p, 8 + EDGE : 8 + EDGE + rows, :]


def backward(mine, rows, count, heard, wave, lap, bent, model, image, adjoint, weighted, gain):
    nx, tall, depth = bent.shape
    shot = lax.axis_index("shot")
    core = lax.rem(shot, 2)
    half = rows // 2
    wide = half + 2 * EDGE
    first = pl.multiple_of((core if mine else 1 - core) * half, 8)
    some = 40 if wide % 40 == 0 else 16
    low, high = edges(some, depth)

    def at(a, size=some, off=0):
        return pl.ds(pl.multiple_of(first + (a + off), 8), size)

    for a in range(0, wide, some):
        here = slice(a, a + some)
        for x in range(nx):
            now = count[at(a, off=x * tall), :] * wave[NT - 1, x, at(a, off=8), :] - heard[NT - 1, at(a, off=x * tall), :]
            adjoint[NT % 2, x, here, :] = now
            weighted[NT % 2, x, 8 + a : 8 + a + some, :] = now * model[x, at(a, off=8), :]
            gain[x, here, :] = now * lap[NT - 2, x, at(a), :]

    for level in range(NT - 1, 1, -1):
        new, old = level % 2, 1 - level % 2
        for a in range(0, wide, some):
            here = slice(a, a + some)
            for x, held in sweep(weighted, (old,), 8 + a, some, nx):
                turn = bend(weighted, (old,), 8 + a, some, nx, x, held, low, high) - 6.0 * held[1]
                after = adjoint[old, x, here, :]
                now = count[at(a, off=x * tall), :] * wave[level - 1, x, at(a, off=8), :]
                now = (now - heard[level - 1, at(a, off=x * tall), :]) + (turn + (after + after))
                if level < NT - 1:
                    now = now - adjoint[new, x, here, :]
                adjoint[new, x, here, :] = now
                weighted[new, x, 8 + a : 8 + a + some, :] = now * model[x, at(a, off=8), :]
                gain[x, here, :] = gain[x, here, :] + now * lap[level - 2, x, at(a), :]

    some = 32 if half % 32 == 0 else 16
    low, high = edges(some, depth)
    for a in range(EDGE, EDGE + half, some):
        here = slice(a, a + some)
        for x, held in sweep(weighted, (0,), 8 + a, some, nx):
            turn = bend(weighted, (0,), 8 + a, some, nx, x, held, low, high) - 6.0 * held[1]
            after = adjoint[0, x, here, :]
            now = count[at(a, some, x * tall), :] * wave[0, x, at(a, some, 8), :]
            now = (now - heard[0, at(a, some, x * tall), :]) + (turn + (after + after)) - adjoint[1, x, here, :]
            total = gain[x, here, :] + now * bent[x, at(a, some), :]
            image[x * half + a - EDGE : x * half + a - EDGE + some, :] = total / NT

    @pl.when(shot == 0)
    def _():
        for x in range(nx):
            weighted[0, x, 0 : wide + 16, :] = model[x, pl.ds(first, wide + 16), :]
        for a in range(EDGE, EDGE + half, some):
            for x, held in sweep(weighted, (0,), 8 + a, some, nx):
                total = bend(weighted, (0,), 8 + a, some, nx, x, held, low, high)
                score = (total / 6.0 - held[1]) * PRIOR_GAIN
                to = slice(x * half + a - EDGE, x * half + a - EDGE + some)
                image[to, :] = image[to, :] - score


def cut(blocks, keep, got, *outs):
    dom = lax.axis_index("dom")
    size = outs[0].shape[0]
    for s in range(blocks):
        at = pl.ds(pl.multiple_of(lax.bitwise_xor(dom, s) * size, 8), size)
        outs[s][...] = keep[at, :] + got[at, :]


def sort(blocks, *refs):
    came, outs, held = refs[:blocks][::-1], refs[blocks : 2 * blocks], refs[2 * blocks]
    dom, pair = lax.axis_index("dom"), lax.axis_index("shot") // 2
    for s in range(blocks):
        held[lax.bitwise_xor(dom, s)] = came[s][...]
    for s in range(blocks):
        outs[s][...] = held[lax.bitwise_xor(pair, s)]


def add(planes, *refs):
    out = refs[-1]
    size = out.shape[1]
    for p in range(planes):
        total = refs[0][p * size : (p + 1) * size, :]
        for ref in refs[1:-1]:
            total = total + ref[p * size : (p + 1) * size, :]
        out[p] = total


def join(planes, rows, *refs):
    out = refs[-1]
    dom = lax.axis_index("dom")
    for s, ref in enumerate(refs[:-1]):
        at = pl.ds(pl.multiple_of(lax.bitwise_xor(dom, s) * rows, 8), rows)
        for p in range(planes):
            out[p, at, :] = ref[p * rows : (p + 1) * rows, :]


def shards(kappa, wave_now, wave_before, wavelet, source_cell, receiver_cells, observed):
    shots, blocks = lax.axis_size("shot"), lax.axis_size("dom")
    _, planes, ny, depth = wave_now.shape
    rows = ny // blocks
    tall = rows + 2 * EDGE
    nx = planes * blocks
    listed = receiver_cells.shape[1]

    def across(array, to):
        pairs = []
        for shot in range(shots):
            for dom in range(blocks):
                there = to(shot, dom)
                pairs.append((shot * blocks + dom, there[0] * blocks + there[1]))
        return lax.ppermute(array, ("shot", "dom"), pairs)

    def over_dom(arrays):
        return [arrays[0]] + [across(arrays[s], lambda shot, dom, s=s: (shot, dom ^ s)) for s in range(1, blocks)]

    def over_pairs(arrays):
        return [arrays[0]] + [across(arrays[s], lambda shot, dom, s=s: (shot ^ (2 * s), dom)) for s in range(1, blocks)]

    half = tall // 2
    held = pltpu.VMEM((planes, ny, depth), jnp.float32)
    early = call(
        functools.partial(pack_early, blocks, planes, rows),
        [(planes * (tall + half), depth)] * (blocks - 1),
        in_specs=[HBM] * 2,
        scratch=[
            held,
            pltpu.VMEM((planes, blocks, rows // 2, depth), jnp.float32),
            pltpu.VMEM((planes, blocks, EDGE, depth), jnp.float32),
            pltpu.SemaphoreType.DMA((planes + 2,)),
        ],
    )(stay(kappa.reshape(planes, blocks, rows, depth)), stay(wave_now[0]))
    early, before = lax.optimization_barrier((early, wave_before[0]))
    *late, own = call(
        functools.partial(pack_late, blocks, planes, rows),
        [(planes * tall, depth)] * (blocks - 1) + [(3 * planes * tall, depth)],
        in_specs=[HBM] * 3,
        scratch=[held, held, held, pltpu.SemaphoreType.DMA((3, planes))],
    )(stay(kappa), stay(wave_now[0]), stay(before))
    early = over_dom([None, *early])[1:]
    late = over_dom([None, *late])[1:]

    count, heard, pulse = call(
        functools.partial(spread, depth, ny, rows, listed),
        [(nx * tall, depth), (NT, nx * tall, depth), (NT, depth)],
        in_specs=[SMEM, HBM, HBM, HBM],
        scratch=[pltpu.VMEM((listed + BLOCK, depth), jnp.float32)]
        + [pltpu.VMEM(array.shape, array.dtype) for array in (wavelet, receiver_cells, observed)]
        + [pltpu.SemaphoreType.DMA((3,))],
        flops=600 * 1000 * 1000,
        moved=1,
    )(source_cell, stay(wavelet), stay(receiver_cells), stay(observed))

    came, pulse = lax.optimization_barrier((early, pulse))
    parts = call(
        functools.partial(gather, planes, half), [((blocks - 1) * half, depth)] * planes, in_specs=[VMEM] * (blocks - 1)
    )(*came)
    swapped = [across(part, lambda shot, dom: (shot ^ 1, dom)) for part in parts]

    padded, plain = (nx, tall + 16, depth), (nx, tall, depth)
    cells = nx * tall * depth
    start, bent, model, step = call(
        functools.partial(begin, blocks, planes, rows),
        [padded, plain, padded, plain],
        in_specs=[VMEM] * (blocks + planes),
        flops=1,
        moved=1,
    )(own, *early, *swapped)
    wave, lap, *turned = call(
        functools.partial(forward, blocks, planes, rows, ny),
        [(NT, *padded), (NT - 1, *plain)] + [(planes * rows, depth)] * blocks,
        in_specs=[SMEM] + [VMEM] * (blocks + 4),
        flops=16 * NT * cells,
        moved=16 * NT * cells,
    )(source_cell, pulse, *late, own, start, model, step)
    half = rows // 2
    side = half + 2 * EDGE
    give, keep = (
        call(
            functools.partial(backward, mine, rows),
            [(nx * half, depth)],
            in_specs=[VMEM] * 6,
            scratch=[
                pltpu.VMEM((2, nx, side, depth), jnp.float32),
                pltpu.VMEM((2, nx, side + 16, depth), jnp.float32),
                pltpu.VMEM((nx, side, depth), jnp.float32),
            ],
            flops=12 * NT * cells,
            moved=12 * NT * cells,
        )(count, heard, wave, lap, bent, model)[0]
        for mine in (False, True)
    )

    got = across(give, lambda shot, dom: (shot ^ 1, dom))
    pieces = call(functools.partial(cut, blocks), [(planes * half, depth)] * blocks, in_specs=[VMEM] * 2)(keep, got)
    pieces = over_dom(pieces)
    turned = over_dom(turned)
    pieces = call(
        functools.partial(sort, blocks),
        [(planes * half, depth)] * blocks,
        in_specs=[VMEM] * blocks,
        scratch=[pltpu.VMEM((blocks, planes * half, depth), jnp.float32)],
        flops=1400 * 1000 * 1000,
        moved=1,
    )(*pieces[::-1])
    pieces = over_pairs(pieces)
    (wave_next,) = call(functools.partial(join, planes, rows), [(planes, ny, depth)], in_specs=[VMEM] * blocks)(*turned)
    (total,) = call(functools.partial(add, planes), [(planes, half, depth)], in_specs=[VMEM] * blocks)(*pieces[::-1])
    return total, wave_next[None]


def solution(mesh):
    return jax.shard_map(
        shards,
        mesh=mesh,
        in_specs=(
            P("dom", None, None),
            P("shot", "dom", None, None),
            P("shot", "dom", None, None),
            P("shot", None),
            P("shot"),
            P("shot", None),
            P("shot", None, None),
        ),
        out_specs=(P("dom", "shot", None), P("shot", "dom", None, None)),
        check_vma=False,
    )
```

```python
import functools

import jax
import jax.numpy as jnp
from jax import lax
from jax.experimental import pallas as pl
from jax.experimental.pallas import tpu as pltpu
from jax.sharding import PartitionSpec as P

NT = 4
PRIOR_GAIN = 50.0
EDGE = 8
VMEM = pl.BlockSpec(memory_space=pltpu.VMEM)
HBM = pl.BlockSpec(memory_space=pltpu.HBM)
SMEM = pl.BlockSpec(memory_space=pltpu.SMEM)
LIMIT = 32 * 1024 * 1024
BLOCK = 768


def stay(array):
    return pltpu.with_memory_space_constraint(array, pltpu.HBM)


def call(body, out_rows, scratch=(), in_specs=(), flops=0, moved=0):
    return pl.pallas_call(
        body,
        out_shape=[jax.ShapeDtypeStruct(*s) if isinstance(s[0], tuple) else jax.ShapeDtypeStruct(s, jnp.float32) for s in out_rows],
        in_specs=list(in_specs),
        out_specs=[VMEM] * len(out_rows),
        scratch_shapes=list(scratch),
        compiler_params=pltpu.CompilerParams(vmem_limit_bytes=LIMIT),
        cost_estimate=pl.CostEstimate(flops=flops, bytes_accessed=moved, transcendentals=0),
    )


def window(field, plane, block, blocks, rows):
    first = pl.multiple_of(block * rows, 8)
    above = pl.multiple_of(jnp.maximum(first - EDGE, 0), 8)
    below = pl.multiple_of(jnp.minimum(first + rows, (blocks * rows) - EDGE), 8)
    top = field[plane, pl.ds(above, EDGE), :]
    bottom = field[plane, pl.ds(below, EDGE), :]
    top = jnp.where(block > 0, top, 0.0)
    bottom = jnp.where(block < blocks - 1, bottom, 0.0)
    return top, field[plane, pl.ds(first, rows), :], bottom


def put(field, plane, block, blocks, rows, out, at):
    top, core, bottom = window(field, plane, block, blocks, rows)
    out[at : at + EDGE, :] = top
    out[at + EDGE : at + EDGE + rows, :] = core
    out[at + EDGE + rows : at + rows + 2 * EDGE, :] = bottom


def fetch(field, held, semaphores):
    copies = [pltpu.make_async_copy(field.at[p], held.at[p], semaphores.at[p]) for p in range(held.shape[0])]
    for copy in copies:
        copy.start()
    return copies


def pack_early(blocks, planes, rows, kappa, now, *refs):
    outs, (held, inner, outer, semaphores) = refs[: blocks - 1], refs[blocks - 1 :]
    dom, core = lax.axis_index("dom"), lax.rem(lax.axis_index("shot"), 2)
    tall, side = rows + 2 * EDGE, rows // 2
    half = side + EDGE
    inside = pl.ds(pl.multiple_of(core * side, 8), side)
    beside = pl.ds(pl.multiple_of((1 - core) * (rows - EDGE), 8), EDGE)
    copies = fetch(now, held, semaphores)
    copies.append(pltpu.make_async_copy(kappa.at[:, :, inside], inner, semaphores.at[planes]))
    copies.append(pltpu.make_async_copy(kappa.at[:, :, beside], outer, semaphores.at[planes + 1]))
    for copy in copies[planes:]:
        copy.start()
    for p in range(planes):
        copies[p].wait()
        for s in range(1, blocks):
            put(held, p, lax.bitwise_xor(dom, s), blocks, rows, outs[s - 1], p * tall)
    for copy in copies[planes:]:
        copy.wait()
    for s in range(1, blocks):
        block = lax.bitwise_xor(dom, s)
        next_to = block - 1 + 2 * core
        there = (next_to >= 0) & (next_to < blocks)
        next_to = jnp.clip(next_to, 0, blocks - 1)
        for p in range(planes):
            at = planes * tall + p * half
            inner_at = pl.ds(pl.multiple_of(at + EDGE * (1 - core), 8), side)
            outer_at = pl.ds(pl.multiple_of(at + side * core, 8), EDGE)
            outs[s - 1][inner_at, :] = inner[p, block]
            outs[s - 1][outer_at, :] = jnp.where(there, outer[p, next_to], 0.0)


def pack_late(blocks, planes, rows, kappa, now, before, *refs):
    outs, own, refs = refs[: blocks - 1], refs[blocks - 1], refs[blocks:]
    held, semaphores = refs[:3], refs[3]
    copies = [fetch(field, ref, semaphores.at[i]) for i, (field, ref) in enumerate(zip((before, now, kappa), held))]
    dom = lax.axis_index("dom")
    tall = rows + 2 * EDGE
    for f in range(3):
        for p in range(planes):
            copies[f][p].wait()
            put(held[f], p, dom, blocks, rows, own, (f * planes + p) * tall)
            if f == 0:
                for s in range(1, blocks):
                    put(held[f], p, lax.bitwise_xor(dom, s), blocks, rows, outs[s - 1], p * tall)


def gather(planes, half, *refs):
    parts, outs = refs[:-planes], refs[-planes:]
    for i, part in enumerate(parts):
        first = part.shape[0] - planes * half
        for p, out in enumerate(outs):
            out[i * half : (i + 1) * half, :] = part[first + p * half : first + (p + 1) * half, :]


def spread(depth, ny, rows, count, source, lists_at, cells_at, observed_at, *refs):
    count_ref, heard_ref, pulse_ref, listed, wavelet, cells_ref, observed_ref, semaphores = refs
    copies = [
        pltpu.make_async_copy(lists_at, wavelet, semaphores.at[0]),
        pltpu.make_async_copy(cells_at, cells_ref, semaphores.at[1]),
        pltpu.make_async_copy(observed_at, observed_ref, semaphores.at[2]),
    ]
    for copy in copies:
        copy.start()
    tall = rows + 2 * EDGE
    size = count_ref.shape[0]
    dom = lax.axis_index("dom")
    spot = lax.rem(source[0], depth)
    lane = lax.broadcasted_iota(jnp.int32, (1, depth), 1)
    count_ref[...] = jnp.zeros_like(count_ref)
    heard_ref[...] = jnp.zeros_like(heard_ref)
    for copy in copies:
        copy.wait()
    for n in range(NT):
        pulse_ref[n : n + 1, :] = jnp.where(lane == spot, wavelet[:, n : n + 1], 0.0)
    cells = cells_ref[...]
    line = cells // depth
    x = line // ny
    y = line - x * ny - (dom * rows - EDGE)
    here = (y >= 0) & (y < tall)
    row = x * tall + jnp.clip(y, 0, tall - 1)
    coarse = row // 64
    stack = [array.astype(jnp.float32) for array in (coarse, row - coarse * 64, cells - line * depth)]
    left = observed_ref[0]
    for part in range(3):
        piece = left.astype(jnp.bfloat16).astype(jnp.float32)
        left = left - piece
        stack.append(piece)
    stack = jnp.concatenate(stack + [jnp.zeros((13 - 3 * NT, count), jnp.float32)], axis=0)

    columns = 128
    ones = jnp.where(here, 1.0, 0.0)
    ones = jnp.concatenate([ones[:, j : j + columns] for j in range(0, count, columns)], axis=0)
    square = (columns, columns)
    down, across = lax.broadcasted_iota(jnp.int32, square, 0), lax.broadcasted_iota(jnp.int32, square, 1)
    order = jnp.dot(ones, jnp.where(down < across, 1.0, 0.0), preferred_element_type=jnp.float32)
    order = jnp.where(ones > 0.0, order, -1.0)
    slots = down.astype(jnp.float32)
    total = 0
    for j in range(count // columns):
        turned = stack[:, j * columns : (j + 1) * columns].T.astype(jnp.bfloat16)
        move = jnp.where(slots == order[j : j + 1, :], 1.0, 0.0).astype(jnp.bfloat16)
        listed[pl.ds(total, columns), 0:16] = jnp.dot(move, turned, preferred_element_type=jnp.float32)
        total = total + jnp.sum(ones[j : j + 1, :]).astype(jnp.int32)

    def block(k, _):
        first = pl.multiple_of(k * BLOCK, 8)
        which = lax.broadcasted_iota(jnp.int32, (BLOCK, 16), 0) + first
        some = jnp.where(which < total, listed[pl.ds(first, BLOCK), 0:16], -1.0)
        flat = some.T
        ids = (flat[0:1, :] * 64.0 + flat[1:2, :]).astype(jnp.int32)
        hot = jnp.where(lax.broadcasted_iota(jnp.int32, (size, BLOCK), 0) == ids, 1.0, 0.0).astype(jnp.bfloat16)
        at = lax.broadcasted_iota(jnp.int32, (BLOCK, depth), 1).astype(jnp.float32) == some[:, 2:3]
        at = jnp.where(at, 1.0, 0.0).astype(jnp.bfloat16)
        some = some.astype(jnp.bfloat16)
        value = [at] + [at * some[:, 3 + i : 4 + i] for i in range(3 * NT)]
        out = jnp.dot(hot, jnp.concatenate(value, axis=1), preferred_element_type=jnp.float32)
        count_ref[...] += out[:, 0:depth]
        for n in range(NT):
            high, mid, low = (out[:, i * depth : (i + 1) * depth] for i in (1 + n, 1 + NT + n, 1 + 2 * NT + n))
            heard_ref[n] += high + (mid + low)
        return 0

    lax.fori_loop(0, (total + BLOCK - 1) // BLOCK, block, 0)


def bend(field, at, first, some, nx, x, planes_held, low, high):
    under, mid, over = planes_held
    total = field[(*at, x, pl.ds(first + 1, some))] + field[(*at, x, pl.ds(first - 1, some))]
    up = jnp.where(high, 0.0, pltpu.roll(mid, mid.shape[1] - 1, 1))
    down = jnp.where(low, 0.0, pltpu.roll(mid, 1, 1))
    total = total + (up + down)
    if x > 0:
        total = total + under
    if x < nx - 1:
        total = total + over
    return total


def sweep(field, at, first, some, nx):
    under, mid = None, field[(*at, 0, pl.ds(first, some))]
    for x in range(nx):
        over = field[(*at, x + 1, pl.ds(first, some))] if x < nx - 1 else None
        yield x, (under, mid, over)
        under, mid = mid, over


def edges(some, depth):
    lanes = lax.broadcasted_iota(jnp.int32, (some, depth), 1)
    return lanes == 0, lanes == depth - 1


def begin(blocks, planes, rows, own, *refs):
    early, swapped, (wave, lap, model, step) = refs[: blocks - 1], refs[blocks - 1 : -4], refs[-4:]
    nx, tall, depth = lap.shape
    dom, core = lax.axis_index("dom"), lax.rem(lax.axis_index("shot"), 2)
    half = tall // 2
    near = pl.ds(pl.multiple_of(8 + core * half, 8), half)
    other = pl.ds(pl.multiple_of(8 + (1 - core) * half, 8), half)
    for s in range(blocks):
        first = planes * lax.bitwise_xor(dom, s)
        for p in range(planes):
            if s == 0:
                at = (planes + p) * tall
                wave[first + p, 8 : 8 + tall, :] = own[at : at + tall, :]
                at += planes * tall
                model[first + p, 8 : 8 + tall, :] = own[at : at + tall, :]
            else:
                wave[first + p, 8 : 8 + tall, :] = early[s - 1][p * tall : (p + 1) * tall, :]
                at = planes * tall + p * half
                model[first + p, near, :] = early[s - 1][at : at + half, :]
                model[first + p, other, :] = swapped[p][(s - 1) * half : s * half, :]
    some = 48
    low, high = edges(some, depth)
    for a in range(0, tall, some):
        rows_at = slice(8 + a, 8 + a + some)
        for x, held in sweep(wave, (), 8 + a, some, nx):
            turn = bend(wave, (), 8 + a, some, nx, x, held, low, high) - 6.0 * held[1]
            lap[x, a : a + some, :] = turn
            step[x, a : a + some, :] = (held[1] + held[1]) + model[x, rows_at, :] * turn


def forward(blocks, planes, rows, ny, source, pulse, *refs):
    late, own, start, model, step, refs = refs[: blocks - 1][::-1], *refs[blocks - 1 : blocks + 3], refs[blocks + 3 :]
    wave, lap, turned = *refs[:2], refs[2:]
    nx, tall, depth = lap.shape[1:]
    dom = lax.axis_index("dom")
    some = 48
    low, high = edges(some, depth)
    line = source[0] // depth
    sx = line // ny
    sy = line - sx * ny - (dom * rows - EDGE)
    source_here = (sy >= 0) & (sy < tall)
    sy = 8 + jnp.clip(sy, 0, tall - 1)

    def inject(n):
        @pl.when(source_here)
        def _():
            wave[n, sx, pl.ds(sy, 1), :] = wave[n, sx, pl.ds(sy, 1), :] + pulse[n : n + 1, :]

    for s in range(blocks):
        before = late[s - 1] if s > 0 else own
        for p in range(planes):
            x = planes * lax.bitwise_xor(dom, s) + p
            wave[0, x, 8 : 8 + tall, :] = step[x] - before[p * tall : (p + 1) * tall, :]
    inject(0)

    for n in range(1, NT):
        for a in range(0, tall, some):
            rows_at = slice(8 + a, 8 + a + some)
            for x, held in sweep(wave, (n - 1,), 8 + a, some, nx):
                mid = held[1]
                turn = bend(wave, (n - 1,), 8 + a, some, nx, x, held, low, high) - 6.0 * mid
                lap[n - 1, x, a : a + some, :] = turn
                old = start[x, rows_at, :] if n == 1 else wave[n - 2, x, rows_at, :]
                wave[n, x, rows_at, :] = (mid + mid) - old + model[x, rows_at, :] * turn
        inject(n)

    for s in range(blocks):
        first = planes * lax.bitwise_xor(dom, s)
        for p in range(planes):
            turned[s][p * rows : (p + 1) * rows, :] = wave[NT - 1, first + p, 8 + EDGE : 8 + EDGE + rows, :]


def backward(mine, rows, count, heard, wave, lap, bent, model, image, adjoint, weighted, gain):
    nx, tall, depth = bent.shape
    shot = lax.axis_index("shot")
    core = lax.rem(shot, 2)
    half = rows // 2
    wide = half + 2 * EDGE
    first = pl.multiple_of((core if mine else 1 - core) * half, 8)
    some = 40 if wide % 40 == 0 else 16
    low, high = edges(some, depth)

    def at(a, size=some, off=0):
        return pl.ds(pl.multiple_of(first + (a + off), 8), size)

    for a in range(0, wide, some):
        here = slice(a, a + some)
        for x in range(nx):
            now = count[at(a, off=x * tall), :] * wave[NT - 1, x, at(a, off=8), :] - heard[NT - 1, at(a, off=x * tall), :]
            adjoint[NT % 2, x, here, :] = now
            weighted[NT % 2, x, 8 + a : 8 + a + some, :] = now * model[x, at(a, off=8), :]
            gain[x, here, :] = now * lap[NT - 2, x, at(a), :]

    for level in range(NT - 1, 1, -1):
        new, old = level % 2, 1 - level % 2
        for a in range(0, wide, some):
            here = slice(a, a + some)
            for x, held in sweep(weighted, (old,), 8 + a, some, nx):
                turn = bend(weighted, (old,), 8 + a, some, nx, x, held, low, high) - 6.0 * held[1]
                after = adjoint[old, x, here, :]
                now = count[at(a, off=x * tall), :] * wave[level - 1, x, at(a, off=8), :]
                now = (now - heard[level - 1, at(a, off=x * tall), :]) + (turn + (after + after))
                if level < NT - 1:
                    now = now - adjoint[new, x, here, :]
                adjoint[new, x, here, :] = now
                weighted[new, x, 8 + a : 8 + a + some, :] = now * model[x, at(a, off=8), :]
                gain[x, here, :] = gain[x, here, :] + now * lap[level - 2, x, at(a), :]

    some = 32 if half % 32 == 0 else 16
    low, high = edges(some, depth)
    for a in range(EDGE, EDGE + half, some):
        here = slice(a, a + some)
        for x, held in sweep(weighted, (0,), 8 + a, some, nx):
            turn = bend(weighted, (0,), 8 + a, some, nx, x, held, low, high) - 6.0 * held[1]
            after = adjoint[0, x, here, :]
            now = count[at(a, some, x * tall), :] * wave[0, x, at(a, some, 8), :]
            now = (now - heard[0, at(a, some, x * tall), :]) + (turn + (after + after)) - adjoint[1, x, here, :]
            total = gain[x, here, :] + now * bent[x, at(a, some), :]
            image[x * half + a - EDGE : x * half + a - EDGE + some, :] = total / NT

    @pl.when(shot == 0)
    def _():
        for x in range(nx):
            weighted[0, x, 0 : wide + 16, :] = model[x, pl.ds(first, wide + 16), :]
        for a in range(EDGE, EDGE + half, some):
            for x, held in sweep(weighted, (0,), 8 + a, some, nx):
                total = bend(weighted, (0,), 8 + a, some, nx, x, held, low, high)
                score = (total / 6.0 - held[1]) * PRIOR_GAIN
                to = slice(x * half + a - EDGE, x * half + a - EDGE + some)
                image[to, :] = image[to, :] - score


def cut(blocks, keep, got, *outs):
    dom = lax.axis_index("dom")
    size = outs[0].shape[0]
    for s in range(blocks):
        at = pl.ds(pl.multiple_of(lax.bitwise_xor(dom, s) * size, 8), size)
        outs[s][...] = keep[at, :] + got[at, :]


def sort(blocks, *refs):
    came, outs, held = refs[:blocks][::-1], refs[blocks : 2 * blocks], refs[2 * blocks]
    dom, pair = lax.axis_index("dom"), lax.axis_index("shot") // 2
    for s in range(blocks):
        held[lax.bitwise_xor(dom, s)] = came[s][...]
    for s in range(blocks):
        outs[s][...] = held[lax.bitwise_xor(pair, s)]


def add(planes, *refs):
    out = refs[-1]
    size = out.shape[1]
    for p in range(planes):
        total = refs[0][p * size : (p + 1) * size, :]
        for ref in refs[1:-1]:
            total = total + ref[p * size : (p + 1) * size, :]
        out[p] = total


def join(planes, rows, *refs):
    out = refs[-1]
    dom = lax.axis_index("dom")
    for s, ref in enumerate(refs[:-1]):
        at = pl.ds(pl.multiple_of(lax.bitwise_xor(dom, s) * rows, 8), rows)
        for p in range(planes):
            out[p, at, :] = ref[p * rows : (p + 1) * rows, :]


def shards(kappa, wave_now, wave_before, wavelet, source_cell, receiver_cells, observed):
    shots, blocks = lax.axis_size("shot"), lax.axis_size("dom")
    _, planes, ny, depth = wave_now.shape
    rows = ny // blocks
    tall = rows + 2 * EDGE
    nx = planes * blocks
    listed = receiver_cells.shape[1]

    def across(array, to):
        pairs = []
        for shot in range(shots):
            for dom in range(blocks):
                there = to(shot, dom)
                pairs.append((shot * blocks + dom, there[0] * blocks + there[1]))
        return lax.ppermute(array, ("shot", "dom"), pairs)

    def over_dom(arrays):
        return [arrays[0]] + [across(arrays[s], lambda shot, dom, s=s: (shot, dom ^ s)) for s in range(1, blocks)]

    def over_pairs(arrays):
        return [arrays[0]] + [across(arrays[s], lambda shot, dom, s=s: (shot ^ (2 * s), dom)) for s in range(1, blocks)]

    half = tall // 2
    held = pltpu.VMEM((planes, ny, depth), jnp.float32)
    early = call(
        functools.partial(pack_early, blocks, planes, rows),
        [(planes * (tall + half), depth)] * (blocks - 1),
        in_specs=[HBM] * 2,
        scratch=[
            held,
            pltpu.VMEM((planes, blocks, rows // 2, depth), jnp.float32),
            pltpu.VMEM((planes, blocks, EDGE, depth), jnp.float32),
            pltpu.SemaphoreType.DMA((planes + 2,)),
        ],
    )(stay(kappa.reshape(planes, blocks, rows, depth)), stay(wave_now[0]))
    early, before = lax.optimization_barrier((early, wave_before[0]))
    *late, own = call(
        functools.partial(pack_late, blocks, planes, rows),
        [(planes * tall, depth)] * (blocks - 1) + [(3 * planes * tall, depth)],
        in_specs=[HBM] * 3,
        scratch=[held, held, held, pltpu.SemaphoreType.DMA((3, planes))],
    )(stay(kappa), stay(wave_now[0]), stay(before))
    early = over_dom([None, *early])[1:]
    late = over_dom([None, *late])[1:]

    count, heard, pulse = call(
        functools.partial(spread, depth, ny, rows, listed),
        [(nx * tall, depth), (NT, nx * tall, depth), (NT, depth)],
        in_specs=[SMEM, HBM, HBM, HBM],
        scratch=[pltpu.VMEM((listed + BLOCK, depth), jnp.float32)]
        + [pltpu.VMEM(array.shape, array.dtype) for array in (wavelet, receiver_cells, observed)]
        + [pltpu.SemaphoreType.DMA((3,))],
        flops=600 * 1000 * 1000,
        moved=1,
    )(source_cell, stay(wavelet), stay(receiver_cells), stay(observed))

    came, pulse = lax.optimization_barrier((early, pulse))
    parts = call(
        functools.partial(gather, planes, half), [((blocks - 1) * half, depth)] * planes, in_specs=[VMEM] * (blocks - 1)
    )(*came)
    swapped = [across(part, lambda shot, dom: (shot ^ 1, dom)) for part in parts]

    padded, plain = (nx, tall + 16, depth), (nx, tall, depth)
    cells = nx * tall * depth
    start, bent, model, step = call(
        functools.partial(begin, blocks, planes, rows),
        [padded, plain, padded, plain],
        in_specs=[VMEM] * (blocks + planes),
        flops=1,
        moved=1,
    )(own, *early, *swapped)
    wave, lap, *turned = call(
        functools.partial(forward, blocks, planes, rows, ny),
        [(NT, *padded), (NT - 1, *plain)] + [(planes * rows, depth)] * blocks,
        in_specs=[SMEM] + [VMEM] * (blocks + 4),
        flops=16 * NT * cells,
        moved=16 * NT * cells,
    )(source_cell, pulse, *late[::-1], own, start, model, step)
    half = rows // 2
    side = half + 2 * EDGE
    give, keep = (
        call(
            functools.partial(backward, mine, rows),
            [(nx * half, depth)],
            in_specs=[VMEM] * 6,
            scratch=[
                pltpu.VMEM((2, nx, side, depth), jnp.float32),
                pltpu.VMEM((2, nx, side + 16, depth), jnp.float32),
                pltpu.VMEM((nx, side, depth), jnp.float32),
            ],
            flops=12 * NT * cells,
            moved=12 * NT * cells,
        )(count, heard, wave, lap, bent, model)[0]
        for mine in (False, True)
    )

    got = across(give, lambda shot, dom: (shot ^ 1, dom))
    pieces = call(functools.partial(cut, blocks), [(planes * half, depth)] * blocks, in_specs=[VMEM] * 2)(keep, got)
    pieces = over_dom(pieces)
    turned = over_dom(turned)
    pieces = call(
        functools.partial(sort, blocks),
        [(planes * half, depth)] * blocks,
        in_specs=[VMEM] * blocks,
        scratch=[pltpu.VMEM((blocks, planes * half, depth), jnp.float32)],
        flops=1400 * 1000 * 1000,
        moved=1,
    )(*pieces[::-1])
    pieces = over_pairs(pieces)
    (wave_next,) = call(functools.partial(join, planes, rows), [(planes, ny, depth)], in_specs=[VMEM] * blocks)(*turned)
    (total,) = call(functools.partial(add, planes), [(planes, half, depth)], in_specs=[VMEM] * blocks)(*pieces[::-1])
    return total, wave_next[None]


def solution(mesh):
    return jax.shard_map(
        shards,
        mesh=mesh,
        in_specs=(
            P("dom", None, None),
            P("shot", "dom", None, None),
            P("shot", "dom", None, None),
            P("shot", None),
            P("shot"),
            P("shot", None),
            P("shot", None, None),
        ),
        out_specs=(P("dom", "shot", None), P("shot", "dom", None, None)),
        check_vma=False,
    )
```
